32 devices in a mesh: dp: 4 (over z), ctx: 8 (over y, x, core).
Axes of the slice: x: 2, y: 2, z: 4, core: 2. Of those that a mesh axis runs over, the one named last changes fastest.
Arguments:
- query_in: bfloat16 [4, 2048, 1280], P('dp', 'ctx'), may hold values from -150 to 150
- key_in: bfloat16 [4, 2048, 1280], P('dp', 'ctx'), may hold values from -16 to 16
- value_in: bfloat16 [4, 2048, 1280], P('dp', 'ctx'), may hold values from -6 to 6
- grad_out: bfloat16 [4, 2048, 1280], P('dp', 'ctx'), may hold values from -6 to 6
- key_blocks: int32 [10, 8, 6], P(None, 'ctx'), may hold values from 0 to 15, as said below
- sink_logits: float32 [10], replicated, may hold values from 3 to 8
Outputs:
- grad_query: bfloat16 [4, 2048, 1280], P('dp', 'ctx')
- grad_key: bfloat16 [4, 2048, 1280], P('dp', 'ctx')
- grad_value: bfloat16 [4, 2048, 1280], P('dp', 'ctx')
- grad_sink: float32 [10], replicated
The draws below stay inside these ranges and needn't reach their ends.
Inputs may be any that keep to these rules, and one draw needn't show every extreme that they name: `key_blocks`: block b holds tokens 128 b to 128 b + 127. The 6 entries of one head and segment are distinct, and none falls in the aligned group of 256 tokens that holds the segment. Counting all heads, entries and segments of one aligned group of 256 tokens, at most 9 entries fall in any one other aligned group of 256 tokens, and every group reaches 9 with some other group in every draw.
All inputs are finite; a program needn't handle non-finite values.
Results may differ from the reference program's by a relative error of at most 0.012.
Values may be sent and summed in bfloat16 or wider, within the bound.
No kernel may reach another device: no remote copies, remote signals or barrier semaphores. Data moves between devices by JAX's collectives and lax.ppermute only.
A program may use at most 64 MiB of HBM per device.

```python
import math
import jax
import jax.numpy as jnp
from jax import lax

TOK_DEV = 256
H = 10
HD = 128
BLOCK = 128
SEG_BLOCKS = 2
KR = 6
B = 4
L = 2048
NB = 16
NSEG = 8
SEG_DEV = 1
CAP = 9


def paired_fields(key):
    base_key = jax.random.fold_in(key, 7)
    key_one, key_two = jax.random.split(base_key, 2)
    shape_all = (B, L, H * HD)
    key_field = jnp.clip(jax.random.normal(key_one, shape_all, jnp.float32), -5.0, 5.0)
    query_field = jnp.clip(jax.random.normal(key_two, shape_all, jnp.float32), -5.0, 5.0)
    return (query_field, key_field)


def draw_query_in(key, part):
    return paired_fields(key)[0].astype(jnp.bfloat16)


def draw_key_in(key, part):
    return paired_fields(key)[1].astype(jnp.bfloat16)


def draw_key_blocks(key, part):
    groups = NSEG // SEG_DEV
    per_group = TOK_DEV // BLOCK
    requests = SEG_DEV * H * KR
    key_one, key_two = jax.random.split(jax.random.fold_in(key, 3))
    sources = jnp.arange(groups, dtype=jnp.int32)
    offsets = jnp.arange(groups - 1, dtype=jnp.int32)
    owners_all = (sources[:, None] + 1 + offsets[None, :]) % groups
    ranking = (jax.random.randint(key_one, (groups, groups - 1), 0, groups, dtype=jnp.int32) + owners_all) * groups + offsets[None, :]
    visit_order = jnp.argsort(ranking, axis=1, stable=True).astype(jnp.int32)
    picks = jnp.arange(requests, dtype=jnp.int32) // CAP
    owners = (sources[:, None] + 1 + visit_order[:, picks]) % groups
    within = jax.random.randint(key_two, (groups, requests), 0, per_group, dtype=jnp.int32)
    blocks = owners * per_group + within
    return jnp.transpose(blocks.reshape(groups, KR, H, SEG_DEV), (2, 0, 3, 1)).reshape(H, NSEG, KR)


def block_scale(rng, shape, pieces, smallest, largest):
    gain, own = 1.0, jax.random.fold_in(rng, 6)
    for dim, blocks in pieces:
        heights = jnp.exp(jax.random.uniform(jax.random.fold_in(own, dim), (blocks,), jnp.float32, smallest / len(pieces), largest / len(pieces)))
        gain = gain * jnp.repeat(heights, shape[dim] // blocks).reshape([-1 if axis == dim else 1 for axis in range(len(shape))])
    return gain


def gaussian(stream_key, extent, spread, limit, cuts=(), held_as=jnp.bfloat16):
    entries = jax.random.normal(stream_key, extent, jnp.float32) * spread
    if len(cuts) > 0:
        entries = block_scale(stream_key, extent, cuts, -0.22, 0.18) * entries
    return jnp.clip(entries, min=-limit, max=limit).astype(held_as)


def setup_inputs(seed: int = 0) -> dict:
    arg_keys = jax.random.split(jax.random.key(seed), 7)
    return {
        "query_in": draw_query_in(jax.random.fold_in(arg_keys[6], 71), 0),
        "key_in": draw_key_in(jax.random.fold_in(arg_keys[6], 71), 0),
        "value_in": gaussian(arg_keys[2], (B, L, H * HD), 1.0, 6.0, ((0, 4), (1, 8))),
        "grad_out": gaussian(arg_keys[3], (B, L, H * HD), 1.0, 6.0, ((0, 4), (1, 8))),
        "key_blocks": draw_key_blocks(jax.random.fold_in(arg_keys[6], 71), 0),
        "sink_logits": jnp.clip(jax.random.uniform(arg_keys[5], (H,), jnp.float32, 3.0, 8.0), 3.0, 8.0),
    }


def head_pass(inputs):
    query_h, key_h, value_h, grad_h, block_rows, sink_h = inputs
    seg_len = SEG_BLOCKS * BLOCK
    scaling = 1.0 / math.sqrt(HD)
    block_ids = block_rows.astype(jnp.int32)

    def keyed(field):
        own_part = field.reshape(NSEG, seg_len, HD)
        listed = field.reshape(NB, BLOCK, HD)[block_ids].reshape(NSEG, KR * BLOCK, HD)
        return jnp.concatenate([own_part, listed], axis=1).astype(jnp.float32)
    key_all = keyed(key_h)
    value_all = keyed(value_h)
    query_f = query_h.reshape(NSEG, seg_len, HD).astype(jnp.float32)
    grad_f = grad_h.reshape(NSEG, seg_len, HD).astype(jnp.float32)
    scores = jnp.einsum('sqd,skd->sqk', query_f, key_all) * scaling
    row_top = jnp.maximum(lax.optimization_barrier(jnp.max(scores, axis=-1)), sink_h)
    row_total = jnp.exp(sink_h - row_top) + lax.optimization_barrier(jnp.sum(jnp.exp(scores - row_top[..., None]), axis=-1))
    log_norm = row_top + jnp.log(row_total)
    weights = jnp.exp(scores - log_norm[..., None])
    prob_f = lax.optimization_barrier(weights.astype(jnp.bfloat16)).astype(jnp.float32)
    attended = jnp.einsum('sqk,skd->sqd', prob_f, value_all).astype(jnp.bfloat16)
    attended_f = lax.optimization_barrier(attended).astype(jnp.float32)
    row_delta = lax.optimization_barrier(jnp.sum(grad_f * attended_f, axis=-1))
    dprobs = jnp.einsum('sqd,skd->sqk', grad_f, value_all)
    dscores = weights * (dprobs - row_delta[..., None])
    dscores = lax.optimization_barrier(dscores.astype(jnp.bfloat16)).astype(jnp.float32)
    grad_q = (jnp.einsum('sqk,skd->sqd', dscores, key_all) * scaling).astype(jnp.bfloat16).reshape(L, HD)
    key_terms = jnp.einsum('sqk,sqd->skd', dscores, query_f) * scaling
    value_terms = jnp.einsum('sqk,sqd->skd', prob_f, grad_f)

    def settle(all_terms):
        own_part = all_terms[:, :seg_len].reshape(L, HD)
        listed = lax.optimization_barrier(all_terms[:, seg_len:].astype(jnp.bfloat16)).astype(jnp.float32)
        listed = listed.reshape(NSEG * KR, BLOCK, HD)
        summed = jnp.zeros((NB, BLOCK, HD), jnp.float32).at[block_ids.reshape(-1)].add(listed)
        return (own_part + summed.reshape(L, HD)).astype(jnp.bfloat16)
    sink_part = -jnp.sum(jnp.exp(sink_h - log_norm) * row_delta)
    return (grad_q, settle(key_terms), settle(value_terms), sink_part)

def reference(query_in, key_in, value_in, grad_out, key_blocks, sink_logits):

    def split_heads(field):
        return jnp.transpose(field.reshape(L, H, HD), (1, 0, 2))

    def join_heads(field):
        return jnp.transpose(field, (1, 0, 2)).reshape(L, H * HD)

    def sequence_pass(inputs):
        query_s, key_s, value_s, grad_s = inputs
        grad_q, grad_k, grad_v, sink_parts = lax.map(head_pass, (split_heads(query_s), split_heads(key_s), split_heads(value_s), split_heads(grad_s), key_blocks, sink_logits))
        return (join_heads(grad_q), join_heads(grad_k), join_heads(grad_v), sink_parts)
    grad_query, grad_key, grad_value, sink_all = lax.map(sequence_pass, (query_in, key_in, value_in, grad_out))
    return (grad_query, grad_key, grad_value, lax.optimization_barrier(jnp.sum(sink_all, axis=0)))
```

```python
import math

import jax
import jax.numpy as jnp
from jax import lax
from jax.experimental import pallas as pl
from jax.experimental.pallas import tpu as pltpu
from jax.sharding import PartitionSpec as P

BLOCK = 128
CORES = 2
FAR = -1e30
VMEM_BYTES = 60 * 1024 * 1024
NT = (((1,), (1,)), ((), ()))
NN = (((1,), (0,)), ((), ()))
TN = (((0,), (0,)), ((), ()))


def chunk_sizes(heads):
    first = (heads + 1) // 2
    return (first, heads - first) if heads > first else (first,)


def grid_side(groups):
    side = math.isqrt(groups // CORES)
    assert CORES * side * side == groups
    return side


def moved(index, side, along_query, shift, cross):
    core, col, row = index % CORES, index // CORES % side, index // (CORES * side)
    along_col = (core == 0) == along_query
    if along_col:
        col = (col + shift) % side
    else:
        row = (row + shift) % side
    return (row * side + col) * CORES + (core ^ cross)


def gather_perm(groups, side, along_query, shift, cross):
    return [(moved(i, side, along_query, shift, cross), i) for i in range(groups)]


def return_perm(groups, side, along_query, shift, cross):
    return [(i, moved(i, side, along_query, shift, cross)) for i in range(groups)]


def dot(lhs, rhs, dims):
    return lax.dot_general(lhs, rhs, dims, preferred_element_type=jnp.float32)


def whole(count):
    return [pl.BlockSpec(memory_space=pltpu.VMEM)] * count


def pack_kernel(core_ref, *refs):
    ins, outs = refs[:8], refs[8:]
    for which in range(2):
        for pair in range(2):
            for place in range(2):
                outs[2 * which + pair][place] = ins[4 * which + 2 * pair + place][0]


def pack(core, query_in, grad_out, key_in, value_in, first, heads, half_heads):
    tokens = query_in.shape[1]
    block = (1, tokens, BLOCK)
    mine = pl.BlockSpec(block, lambda h, core: (0, 0, core[0] * half_heads + first + h))
    other = pl.BlockSpec(block, lambda h, core: (0, 0, (1 - core[0]) * half_heads + first + h))
    fields = (query_in, grad_out, key_in, value_in)
    return pl.pallas_call(
        pack_kernel,
        grid_spec=pltpu.PrefetchScalarGridSpec(
            num_scalar_prefetch=1,
            grid=(heads,),
            in_specs=[mine] * 4 + [other] * 4,
            out_specs=[head_spec((2, tokens, BLOCK))] * 4,
        ),
        out_shape=[jax.ShapeDtypeStruct((2, tokens, heads * BLOCK), jnp.bfloat16)] * 4,
        compiler_params=pltpu.CompilerParams(vmem_limit_bytes=VMEM_BYTES),
        cost_estimate=pl.CostEstimate(
            flops=0, bytes_accessed=32 * tokens * heads * BLOCK, transcendentals=0
        ),
        name="pack",
    )(core, *fields, *fields)


def head_spec(shape):
    lead = len(shape) - 1
    return pl.BlockSpec(shape, lambda h, *_: (0,) * lead + (h,))


def stat_spec(rows, tokens):
    return pl.BlockSpec((1, rows, tokens), lambda h, *_: (h, 0, 0))


def spread(refs, firsts, seconds, rows):
    per_slot = refs[0].shape[1] // rows
    for slot, ref in enumerate(refs):
        for part in range(per_slot):
            firsts[slot * per_slot + part] = ref[0, pl.ds(part * rows, rows), :]
            seconds[slot * per_slot + part] = ref[1, pl.ds(part * rows, rows), :]


def paired(ref, one, two):
    return jnp.concatenate([ref[one], ref[two]], axis=0)


def tile_products(tile, bound, base, lists, held, scores, dprobs):
    slot_ref, one_ref, two_ref = lists
    queries, grad_outs, keys, values = held
    place = base + jnp.minimum(tile, bound - 1)
    slot, one, two = slot_ref[place], one_ref[place], two_ref[place]
    raw = dot(paired(keys, one, jnp.maximum(two, 0)), queries[slot], NT)
    scores[:BLOCK] = raw[:BLOCK]
    scores[BLOCK:] = raw[BLOCK:] + jnp.where((two >= 0) & (tile < bound), 0.0, FAR)
    dprobs[...] = dot(paired(values, one, jnp.maximum(two, 0)), grad_outs[slot], NT)


def walk(count, products, work, even, odd):
    products(0, *even)

    def step(index, carry):
        tile = 2 * index
        products(tile + 1, *odd)
        work(tile, *even)
        products(tile + 2, *even)

        @pl.when(tile + 1 < count)
        def _():
            work(tile + 1, *odd)

        return carry

    lax.fori_loop(0, (count + 1) // 2, step, 0)


def stats_kernel(first, slots, most, scaling, cnt_ref, slot_ref, one_ref, two_ref, sink_ref, *refs):
    qd_refs, kv_refs = refs[:slots], refs[slots : 2 * slots]
    out_ref, keys, values, queries, grad_outs, rows, *buffers = refs[2 * slots :]
    head = pl.program_id(0) + first
    tokens = qd_refs[0].shape[1]
    spread(kv_refs, keys, values, BLOCK)
    spread(qd_refs, queries, grad_outs, tokens)
    zero = jnp.zeros((1, tokens), jnp.float32)
    for slot in range(slots):
        rows[slot, 0:1, :] = zero + sink_ref[head]
        rows[slot, 1:2, :] = zero
        rows[slot, 2:3, :] = zero
    base = head * most
    count = cnt_ref[head]
    lists = (slot_ref, one_ref, two_ref)
    held = (queries, grad_outs, keys, values)

    def products(tile, scores, dprobs):
        tile_products(tile, count, base, lists, held, scores, dprobs)

    def work(tile, scores, dprobs):
        slot = slot_ref[base + tile]
        old = rows[slot, 0:1, :]
        top = jnp.maximum(old, jnp.max(scores[...], axis=0, keepdims=True) * scaling)
        parts = jnp.exp(scores[...] * scaling - top)
        shrink = jnp.exp(old - top)
        rows[slot, 0:1, :] = top
        rows[slot, 1:2, :] = rows[slot, 1:2, :] * shrink + jnp.sum(parts, axis=0, keepdims=True)
        rows[slot, 2:3, :] = rows[slot, 2:3, :] * shrink + jnp.sum(
            parts * dprobs[...], axis=0, keepdims=True
        )

    walk(count, products, work, buffers[:2], buffers[2:])
    for slot in range(slots):
        for kind in range(3):
            out_ref[0, pl.ds(kind * slots + slot, 1), :] = rows[slot, kind : kind + 1, :]


def tile_scratch(slots, tokens):
    blocks = slots * (tokens // BLOCK)
    return [pltpu.VMEM((blocks, BLOCK, BLOCK), jnp.bfloat16)] * 2 + [
        pltpu.VMEM((slots, tokens, BLOCK), jnp.bfloat16)
    ] * 2


def tile_buffers(tokens):
    return [pltpu.VMEM((2 * BLOCK, tokens), jnp.float32)] * 4


def stats(lists, sink, qd, kv, first, heads, most, scaling):
    slots, tokens = len(qd), qd[0].shape[1]
    rows = -(-3 * slots // 8) * 8
    tiles = heads * slots * 4
    return pl.pallas_call(
        lambda *refs: stats_kernel(first, slots, most, scaling, *refs),
        grid_spec=pltpu.PrefetchScalarGridSpec(
            num_scalar_prefetch=5,
            grid=(heads,),
            in_specs=[head_spec((2, tokens, BLOCK))] * (2 * slots),
            out_specs=stat_spec(rows, tokens),
            scratch_shapes=tile_scratch(slots, tokens)
            + [pltpu.VMEM((slots, 8, tokens), jnp.float32)]
            + tile_buffers(tokens),
        ),
        out_shape=jax.ShapeDtypeStruct((heads, rows, tokens), jnp.float32),
        compiler_params=pltpu.CompilerParams(vmem_limit_bytes=VMEM_BYTES),
        cost_estimate=pl.CostEstimate(
            flops=tiles * 4 * tokens * BLOCK * BLOCK,
            bytes_accessed=heads * slots * 8 * tokens * BLOCK,
            transcendentals=tiles * tokens * BLOCK,
        ),
        name="row_stats",
    )(*lists, sink, *qd, *kv)


def settle(stat_refs, slot, slots, sink):
    side = len(stat_refs)
    parts = []
    for shift, ref in enumerate(stat_refs):
        place = (slot // CORES - shift) % side * CORES + slot % CORES
        parts.append([ref[0, pl.ds(kind * slots + place, 1), :] for kind in range(3)])
    top = parts[0][0]
    for part in parts[1:]:
        top = jnp.maximum(top, part[0])
    total, mixed = jnp.exp(sink - top), jnp.zeros_like(top)
    for part in parts:
        grow = jnp.exp(part[0] - top)
        total = total + part[1] * grow
        mixed = mixed + part[2] * grow
    return top + jnp.log(total), mixed / total


def grads_kernel(
    first, slots, side, most, scaling, cnt_ref, slot_ref, one_ref, two_ref, sink_ref, *refs
):
    qd_refs, kv_refs = refs[:slots], refs[slots : 2 * slots]
    stat_refs = refs[2 * slots : 2 * slots + side]
    rest = refs[2 * slots + side :]
    remote = slots - CORES
    dq_home, dkv_home, core_out = rest[:3]
    dq_out, dkv_out = rest[3 : 3 + remote], rest[3 + remote : 3 + 2 * remote]
    sink_out = rest[3 + 2 * remote]
    keys, values, queries, grad_outs, rows, dkeys, dvalues, dquery, *buffers = rest[4 + 2 * remote :]
    head = pl.program_id(0) + first
    tokens = qd_refs[0].shape[1]
    spread(kv_refs, keys, values, BLOCK)
    spread(qd_refs, queries, grad_outs, tokens)
    sink = sink_ref[head]
    dkeys[...] = jnp.zeros_like(dkeys)
    dvalues[...] = jnp.zeros_like(dvalues)
    dquery[...] = jnp.zeros_like(dquery)
    sink_row = jnp.zeros((1, tokens), jnp.float32)
    for slot in range(slots):
        log_norm, row_delta = settle(stat_refs, slot, slots, sink)
        rows[slot, 0:1, :] = log_norm
        rows[slot, 1:2, :] = row_delta
        if slot < CORES:
            sink_row = sink_row - jnp.exp(sink - log_norm) * row_delta
    sink_out[0] = jnp.broadcast_to(sink_row, sink_out.shape[1:])
    base = head * most
    count = cnt_ref[head]
    lists = (slot_ref, one_ref, two_ref)
    held = (queries, grad_outs, keys, values)

    def products(tile, scores, dprobs):
        tile_products(tile, count, base, lists, held, scores, dprobs)

    def work(tile, scores, dprobs):
        slot, one = slot_ref[base + tile], one_ref[base + tile]
        two = jnp.maximum(two_ref[base + tile], 0)
        weights = jnp.exp(scores[...] * scaling - rows[slot, 0:1, :])
        probs = weights.astype(jnp.bfloat16)
        dscores = (weights * (dprobs[...] - rows[slot, 1:2, :])).astype(jnp.bfloat16)
        dquery[slot] += dot(paired(keys, one, two), dscores, TN)
        dkey = dot(dscores, queries[slot], NN)
        dvalue = dot(probs, grad_outs[slot], NN)
        dkeys[one] += dkey[:BLOCK]
        dkeys[two] += dkey[BLOCK:]
        dvalues[one] += dvalue[:BLOCK]
        dvalues[two] += dvalue[BLOCK:]

    walk(count, products, work, buffers[:2], buffers[2:])
    for slot in range(slots):
        total = dquery[slot].T * scaling
        if slot == 0:
            dq_home[...] = total
        elif slot < CORES:
            core_out[0] = total.astype(jnp.bfloat16)
        else:
            dq_out[slot - CORES][...] = total.astype(jnp.bfloat16)
    per_slot = tokens // BLOCK
    for slot in range(slots):
        for part in range(per_slot):
            span = pl.ds(part * BLOCK, BLOCK)
            dkey = dkeys[slot * per_slot + part] * scaling
            dvalue = dvalues[slot * per_slot + part]
            if slot == 0:
                dkv_home[0, span, :] = dkey
                dkv_home[1, span, :] = dvalue
            else:
                ref = core_out if slot < CORES else dkv_out[slot - CORES]
                lead = 1 if slot < CORES else 0
                ref[lead, span, :] = dkey.astype(jnp.bfloat16)
                ref[lead + 1, span, :] = dvalue.astype(jnp.bfloat16)


def grads(lists, sink, qd, kv, partials, first, heads, most, scaling):
    slots, tokens = len(qd), qd[0].shape[1]
    side, rows = len(partials), partials[0].shape[1]
    remote = slots - CORES
    blocks = slots * (tokens // BLOCK)
    tiles = heads * slots * 4
    width = heads * BLOCK
    low, high = jnp.bfloat16, jnp.float32
    one, two, three = (tokens, BLOCK), (2, tokens, BLOCK), (3, tokens, BLOCK)
    shapes = [(one, high), (two, high), (three, low)] + [(one, low)] * remote + [(two, low)] * remote
    return pl.pallas_call(
        lambda *refs: grads_kernel(first, slots, side, most, scaling, *refs),
        grid_spec=pltpu.PrefetchScalarGridSpec(
            num_scalar_prefetch=5,
            grid=(heads,),
            in_specs=[head_spec(two)] * (2 * slots) + [stat_spec(rows, tokens)] * side,
            out_specs=[head_spec(shape) for shape, _ in shapes] + [stat_spec(8, tokens)],
            scratch_shapes=tile_scratch(slots, tokens)
            + [pltpu.VMEM((slots, 8, tokens), high)]
            + [pltpu.VMEM((blocks, BLOCK, BLOCK), high)] * 2
            + [pltpu.VMEM((slots, BLOCK, tokens), high)]
            + tile_buffers(tokens),
        ),
        out_shape=[jax.ShapeDtypeStruct(shape[:-1] + (width,), kind) for shape, kind in shapes]
        + [jax.ShapeDtypeStruct((heads, 8, tokens), high)],
        compiler_params=pltpu.CompilerParams(vmem_limit_bytes=VMEM_BYTES),
        cost_estimate=pl.CostEstimate(
            flops=tiles * 10 * tokens * BLOCK * BLOCK,
            bytes_accessed=heads * slots * 16 * tokens * BLOCK,
            transcendentals=tiles * tokens * BLOCK,
        ),
        name="gradients",
    )(*lists, sink, *qd, *kv, *partials)


def close_kernel(sizes, side, half, core_ref, *refs):
    per = 3 + 4 * (side - 1)
    outs = refs[per * len(sizes) :]
    core = core_ref[0]
    first = 0
    for chunk, heads in enumerate(sizes):
        width = heads * BLOCK
        dq_home, dkv_home, from_core, *far = refs[per * chunk : per * (chunk + 1)]
        dq_far, dkv_far = far[: 2 * (side - 1)], far[2 * (side - 1) :]
        mine = pl.ds(pl.multiple_of(core * half + first, BLOCK), width)
        other = pl.ds(pl.multiple_of((1 - core) * half + first, BLOCK), width)
        for place, out in enumerate(outs):
            if place == 0:
                parts = [dq_home[...], from_core[0]] + [ref[...] for ref in dq_far]
            else:
                parts = [dkv_home[place - 1], from_core[place]] + [ref[place - 1] for ref in dkv_far]
            parts = [part.astype(jnp.float32) for part in parts]
            out[0, :, mine] = sum(parts[2::2], parts[0]).astype(jnp.bfloat16)
            out[0, :, other] = sum(parts[3::2], parts[1]).astype(jnp.bfloat16)
        first += width


def close(core, pieces, sizes, side, half, tokens):
    flat = [piece for chunk in pieces for piece in chunk]
    return pl.pallas_call(
        lambda *refs: close_kernel(sizes, side, half, *refs),
        in_specs=[pl.BlockSpec(memory_space=pltpu.SMEM)] + whole(len(flat)),
        out_specs=whole(3),
        out_shape=[jax.ShapeDtypeStruct((1, tokens, 2 * half), jnp.bfloat16)] * 3,
        compiler_params=pltpu.CompilerParams(vmem_limit_bytes=VMEM_BYTES),
        cost_estimate=pl.CostEstimate(
            flops=tokens * half * 12, bytes_accessed=tokens * half * 42, transcendentals=0
        ),
        name="closing_sums",
    )(core, *flat)


def tile_lists(rows, key_devs, per_group):
    heads, slots, listed = rows.shape
    hit = (rows // per_group)[..., None] == key_devs
    slot_ids = jnp.arange(slots, dtype=jnp.int32)
    places = jnp.sum(jnp.where(hit, slot_ids * per_group, 0), axis=-1) + rows % per_group
    found = jnp.any(hit, axis=-1)
    ahead = jnp.arange(listed)[None, :] < jnp.arange(listed)[:, None]
    before = jnp.sum((ahead & found[..., None, :]).astype(jnp.int32), axis=-1)
    own = jnp.where(slot_ids < CORES, per_group // 2, 0)
    needs = own + (jnp.sum(found.astype(jnp.int32), axis=-1) + 1) // 2
    upto = jnp.sum(jnp.where(slot_ids[None, :] <= slot_ids[:, None], needs[:, None, :], 0), axis=-1)
    start = upto - needs
    most = slots * ((listed + 1) // 2) + CORES * (per_group // 2)
    target = jnp.arange(most, dtype=jnp.int32)
    tiles = (start + own)[..., None] + before // 2
    meet = (found[..., None] & (tiles[..., None] == target)).astype(jnp.int32)
    even = (before % 2 == 0).astype(jnp.int32)
    ones = jnp.sum(meet * (places * even)[..., None], axis=(1, 2))
    twos = jnp.sum(meet * ((places + 1) * (1 - even))[..., None], axis=(1, 2)) - 1
    for slot in range(CORES):
        step = target[None, :] - start[:, slot : slot + 1]
        home = (step >= 0) & (step < per_group // 2)
        ones = ones + jnp.where(home, slot * per_group + 2 * step, 0)
        twos = twos + jnp.where(home, slot * per_group + 2 * step + 2, 0)
    where_to = jnp.sum((upto[:, None, :] <= target[None, :, None]).astype(jnp.int32), axis=-1)
    where_to = jnp.minimum(where_to, slots - 1)
    flat = (where_to.reshape(-1), ones.reshape(-1), twos.reshape(-1))
    return (upto[:, -1],) + flat, most


def key_devices(me, side):
    core, col, row = me % CORES, me // CORES % side, me // (CORES * side)
    shifts = jnp.arange(side, dtype=jnp.int32)[:, None]
    cores = core ^ jnp.arange(CORES, dtype=jnp.int32)[None, :]
    by_col = (row * side + (col + shifts) % side) * CORES + cores
    by_row = ((row + shifts) % side * side + col) * CORES + cores
    return jnp.where(core == 0, by_row, by_col).reshape(-1)


def spot_sum(part, groups, me):
    copies = lax.axis_size("dp")
    side = grid_side(groups)
    spot = lax.axis_index("dp") * groups + me
    held = jnp.where(jnp.arange(copies * groups)[:, None] == spot, part[None, :], 0.0)
    for axis, perms in (
        ("dp", [[(i, (i + s) % copies) for i in range(copies)] for s in range(1, copies)]),
        ("ctx", [gather_perm(groups, side, True, s, 0) for s in range(1, side)]),
        ("ctx", [gather_perm(groups, side, False, s, 0) for s in range(1, side)]),
        ("ctx", [gather_perm(groups, side, True, 0, 1)]),
    ):
        came = [lax.ppermute(held, axis, perm) for perm in perms]
        held = sum(came, held)
    return jnp.sum(held, axis=0)


def body(query_in, key_in, value_in, grad_out, key_blocks, sink_logits):
    groups = lax.axis_size("ctx")
    side = grid_side(groups)
    head_count = sink_logits.shape[0]
    tokens = query_in.shape[1]
    per_group = tokens // BLOCK
    assert key_blocks.shape[1] == 1 and query_in.shape[2] == head_count * BLOCK
    assert per_group % 2 == 0 and head_count % CORES == 0
    half_heads = head_count // 2
    half = half_heads * BLOCK
    scaling = 1.0 / math.sqrt(BLOCK)
    sizes = chunk_sizes(half_heads)
    me = lax.axis_index("ctx").astype(jnp.int32)
    core = me % CORES
    core_arg = core.reshape(1)
    swap = gather_perm(groups, side, True, 0, 1)
    places = [(shift, cross) for shift in range(1, side) for cross in range(CORES)]

    asked = key_blocks[:, 0, :]
    asked_own = jnp.where(core == 0, asked[:half_heads], asked[half_heads:])
    asked_oth = jnp.where(core == 0, asked[half_heads:], asked[:half_heads])
    rows = [asked_own, lax.ppermute(asked_oth, "ctx", swap)] + [
        lax.ppermute(
            asked_oth if cross else asked_own, "ctx", gather_perm(groups, side, True, shift, cross)
        )
        for shift, cross in places
    ]
    lists, most = tile_lists(jnp.stack(rows, axis=1), key_devices(me, side), per_group)
    sink = jnp.where(core == 0, sink_logits[:half_heads], sink_logits[half_heads:])

    starts = [sum(sizes[:i]) for i in range(len(sizes))]
    qds, kvs = [], []
    for first, heads in zip(starts, sizes):
        qd_own, kv_own, qd_oth, kv_oth = pack(
            core_arg, query_in, grad_out, key_in, value_in, first, heads, half_heads
        )
        qd = [qd_own, lax.ppermute(qd_oth, "ctx", swap)]
        kv = [kv_own, lax.ppermute(kv_oth, "ctx", swap)]
        for shift, cross in places:
            perm = gather_perm(groups, side, True, shift, cross)
            qd.append(lax.ppermute(qd_oth if cross else qd_own, "ctx", perm))
            perm = gather_perm(groups, side, False, shift, cross)
            kv.append(lax.ppermute(kv_oth if cross else kv_own, "ctx", perm))
        qds.append(qd)
        kvs.append(kv)

    pieces, sink_rows = [], []
    for chunk, (first, heads) in enumerate(zip(starts, sizes)):
        qd, kv = qds[chunk], kvs[chunk]
        partial = stats(lists, sink, qd, kv, first, heads, most, scaling)
        partials = [partial] + [
            lax.ppermute(partial, "ctx", gather_perm(groups, side, True, shift, 0))
            for shift in range(1, side)
        ]
        results = grads(lists, sink, qd, kv, partials, first, heads, most, scaling)
        remote = len(places)
        dq_home, dkv_home, core_out = results[:3]
        dq_out, dkv_out = results[3 : 3 + remote], results[3 + remote : 3 + 2 * remote]
        sink_rows.append(jnp.sum(results[-1][:, 0, :], axis=-1))
        back = [
            lax.ppermute(value, "ctx", return_perm(groups, side, along_query, shift, cross))
            for along_query, values in ((True, dq_out), (False, dkv_out))
            for value, (shift, cross) in zip(values, places)
        ]
        pieces.append([dq_home, dkv_home, lax.ppermute(core_out, "ctx", swap)] + back)

    sink_half = jnp.concatenate(sink_rows)
    zeros = jnp.zeros_like(sink_half)
    sink_part = jnp.where(
        core == 0, jnp.concatenate([sink_half, zeros]), jnp.concatenate([zeros, sink_half])
    )
    grad_sink = spot_sum(sink_part, groups, me)
    grad_query, grad_key, grad_value = close(core_arg, pieces, sizes, side, half, tokens)
    return (grad_query, grad_key, grad_value, grad_sink)


def solution(mesh):
    tokens = P("dp", "ctx", None)
    return jax.shard_map(
        body,
        mesh=mesh,
        in_specs=(tokens, tokens, tokens, tokens, P(None, "ctx", None), P()),
        out_specs=(tokens, tokens, tokens, P()),
        check_vma=False,
    )
```

```python
import math

import jax
import jax.numpy as jnp
from jax import lax
from jax.experimental import pallas as pl
from jax.experimental.pallas import tpu as pltpu
from jax.sharding import PartitionSpec as P

BLOCK = 128
CORES = 2
FAR = -1e30
VMEM_BYTES = 24 * 1024 * 1024
FEW_BYTES = 2 * 1024 * 1024
UNROLL = 5
EXTRA = 16
SMALL = pl.CostEstimate(flops=1, bytes_accessed=1, transcendentals=0)
NT = (((1,), (1,)), ((), ()))
NN = (((1,), (0,)), ((), ()))
TN = (((0,), (0,)), ((), ()))


def chunk_sizes(heads):
    first = (heads + 1) // 2
    return (first, heads - first) if heads > first else (first,)


def grid_side(groups):
    side = math.isqrt(groups // CORES)
    assert CORES * side * side == groups
    return side


def moved(index, side, along_query, shift, cross):
    core, col, row = index % CORES, index // CORES % side, index // (CORES * side)
    along_col = (core == 0) == along_query
    if along_col:
        col = (col + shift) % side
    else:
        row = (row + shift) % side
    return (row * side + col) * CORES + (core ^ cross)


def gather_perm(groups, side, along_query, shift, cross):
    return [(moved(i, side, along_query, shift, cross), i) for i in range(groups)]


def return_perm(groups, side, along_query, shift, cross):
    return [(i, moved(i, side, along_query, shift, cross)) for i in range(groups)]


def dot(lhs, rhs, dims):
    return lax.dot_general(lhs, rhs, dims, preferred_element_type=jnp.float32)


def whole(count):
    return [pl.BlockSpec(memory_space=pltpu.VMEM)] * count


def pack_kernel(first, heads, every, half, q_ref, g_ref, k_ref, v_ref, *rest):
    qd_own, kv_own, qd_oth, kv_oth = rest[:4]
    sems = rest[-1]
    fields = (q_ref, g_ref, k_ref, v_ref)
    core = lax.axis_index("ctx") % CORES
    copies = []

    def copy(ref, which, head, out):
        start = (core if which == 0 else 1 - core) * half + head * BLOCK
        columns = pl.ds(pl.multiple_of(start, BLOCK), BLOCK)
        copies.append(pltpu.make_async_copy(ref.at[0, :, columns], out, sems.at[len(copies)]))

    for head in range(heads):
        for which, outs in enumerate(((qd_own, kv_own), (qd_oth, kv_oth))):
            for place, ref in enumerate(fields):
                copy(ref, which, first + head, outs[place // 2].at[head, place % 2])
    for head in range(every):
        for place, ref in enumerate(fields):
            copy(ref, 1, head, rest[4].at[head, place])
    for each in copies:
        each.start()
    for each in copies:
        each.wait()


def pack(fields, first, heads, every, half):
    tokens = fields[0].shape[1]
    shapes = [(heads, 2, tokens, BLOCK)] * 4 + [(every, 4, tokens, BLOCK)] * (every > 0)
    return pl.pallas_call(
        lambda *refs: pack_kernel(first, heads, every, half, *refs),
        in_specs=[pl.BlockSpec(memory_space=pltpu.HBM)] * 4,
        out_specs=whole(len(shapes)),
        out_shape=[jax.ShapeDtypeStruct(shape, jnp.bfloat16) for shape in shapes],
        scratch_shapes=[pltpu.SemaphoreType.DMA((heads * 8 + every * 4,))],
        compiler_params=pltpu.CompilerParams(vmem_limit_bytes=VMEM_BYTES),
        cost_estimate=SMALL,
        name="pack",
    )(*fields)


def spread(spans, slots, refs, query_side, key_side):
    place = 0
    for span, (first, heads) in enumerate(spans):
        here = refs[span * 2 * slots : (span + 1) * 2 * slots]
        qd_refs, kv_refs = here[:slots], here[slots:]
        parts = kv_refs[0].shape[2] // BLOCK
        for head in range(heads):
            for slot in range(slots):
                from_core = slot == 1
                row = head + (first if from_core else 0)
                for kind in range(2):
                    lead = kind + (2 if from_core else 0)
                    query_side[kind][place] = qd_refs[slot][row, kind]
                    for part in range(parts):
                        key_side[kind][place * parts + part] = kv_refs[slot][
                            row, lead, pl.ds(part * BLOCK, BLOCK), :
                        ]
                place += 1


def paired(ref, one, two):
    return jnp.concatenate([ref[one], ref[two]], axis=0)


def tile_products(tile, tiles, query_side, key_side):
    bound = tiles[0]
    real = tile < bound
    code = tiles[1 + jnp.minimum(tile, bound - 1)]
    query, one, two = code & 255, (code >> 8) & 255, (code >> 16) - 1
    both = real & (two >= 0)
    two = jnp.maximum(two, 0)
    raw = dot(paired(key_side[0], one, two), query_side[0][query], NT)
    scores = jnp.concatenate(
        [raw[:BLOCK] + jnp.where(real, 0.0, FAR), raw[BLOCK:] + jnp.where(both, 0.0, FAR)], axis=0
    )
    dprobs = dot(paired(key_side[1], one, two), query_side[1][query], NT)
    return query, one, two, scores, dprobs


def walk(tiles, query_side, key_side, work):
    def step(index, carry):
        made = [
            tile_products(UNROLL * index + i, tiles, query_side, key_side) for i in range(UNROLL)
        ]
        for one in made:
            work(*one)
        return carry

    lax.fori_loop(0, (tiles[0] + UNROLL - 1) // UNROLL, step, 0)


def tile_scratch(heads, slots, tokens):
    query_side = pltpu.VMEM((heads * slots, tokens, BLOCK), jnp.bfloat16)
    key_side = pltpu.VMEM((heads * slots * (tokens // BLOCK), BLOCK, BLOCK), jnp.bfloat16)
    return [query_side] * 2 + [key_side] * 2 + [pltpu.VMEM((heads * slots, 8, tokens), jnp.float32)]


def stats_kernel(first, heads, slots, scaling, tiles, sink_ref, *refs):
    out_ref, q_all, g_all, k_all, v_all, rows = refs[-6:]
    query_side, key_side = (q_all, g_all), (k_all, v_all)
    spread([(first, heads)], slots, refs, query_side, key_side)
    zero = jnp.zeros((1, out_ref.shape[2]), jnp.float32)
    for head in range(heads):
        for slot in range(slots):
            rows[head * slots + slot, 0:1, :] = zero + sink_ref[first + head]
            rows[head * slots + slot, 1:2, :] = zero
            rows[head * slots + slot, 2:3, :] = zero

    def work(query, one, two, scores, dprobs):
        old = rows[query, 0:1, :]
        top = jnp.maximum(old, jnp.max(scores, axis=0, keepdims=True) * scaling)
        parts = jnp.exp(scores * scaling - top)
        shrink = jnp.exp(old - top)
        rows[query, 0:1, :] = top
        rows[query, 1:2, :] = rows[query, 1:2, :] * shrink + jnp.sum(parts, axis=0, keepdims=True)
        rows[query, 2:3, :] = rows[query, 2:3, :] * shrink + jnp.sum(
            parts * dprobs, axis=0, keepdims=True
        )

    walk(tiles, query_side, key_side, work)
    for head in range(heads):
        for slot in range(slots):
            for kind in range(3):
                out_ref[head, pl.ds(kind * slots + slot, 1), :] = rows[
                    head * slots + slot, kind : kind + 1, :
                ]


def stats(tiles, sink, qd, kv, first, heads, scaling):
    slots, tokens = len(qd), qd[0].shape[2]
    rows = -(-3 * slots // 8) * 8
    return pl.pallas_call(
        lambda *refs: stats_kernel(first, heads, slots, scaling, *refs),
        in_specs=[pl.BlockSpec(memory_space=pltpu.SMEM)] * 2 + whole(2 * slots),
        out_specs=whole(1)[0],
        out_shape=jax.ShapeDtypeStruct((heads, rows, tokens), jnp.float32),
        scratch_shapes=tile_scratch(heads, slots, tokens),
        compiler_params=pltpu.CompilerParams(vmem_limit_bytes=VMEM_BYTES),
        cost_estimate=SMALL,
        name="row_stats",
    )(tiles, sink, *qd, *kv)


def settle(parts, sink):
    top = parts[0][0]
    for part in parts[1:]:
        top = jnp.maximum(top, part[0])
    total, mixed = jnp.exp(sink - top), jnp.zeros_like(top)
    for part in parts:
        grow = jnp.exp(part[0] - top)
        total = total + part[1] * grow
        mixed = mixed + part[2] * grow
    return top + jnp.log(total), mixed / total


def stat_place(slot, shift, side):
    return (slot // CORES - shift) % side * CORES + slot % CORES


def stat_rows(refs, head, slot, slots):
    side = len(refs)
    return [
        [ref[head, pl.ds(kind * slots + stat_place(slot, shift, side), 1), :] for kind in range(3)]
        for shift, ref in enumerate(refs)
    ]


def ordered(items, at, side):
    made = []
    for place in range(side):
        value = items[place]
        for own in range(1, side):
            value = jnp.where(at == own, items[(place - own) % side], value)
        made.append(value)
    return made


def coordinates(side):
    rest, core = halved(lax.axis_index("ctx"), CORES)
    row, col = halved(rest, side)
    return core, jnp.where(core == 0, col, row), jnp.where(core == 0, row, col)


def sink_terms(stat_groups, slots, side, sink_ref, at_query):
    lane = lax.broadcasted_iota(jnp.int32, (1, BLOCK), 1)
    terms = jnp.zeros((1, BLOCK), jnp.float32)
    done = 0
    for stat_refs in stat_groups:
        for head in range(stat_refs[0].shape[0]):
            sink = sink_ref[done]
            chips = []
            for shift in range(side):
                total = 0.0
                for cross in range(CORES):
                    rows = stat_rows(stat_refs, head, shift * CORES + cross, slots)
                    kinds = [ordered(kind, at_query, side) for kind in zip(*rows)]
                    log_norm, row_delta = settle(list(zip(*kinds)), sink)
                    total = total + jnp.exp(sink - log_norm) * row_delta
                chips.append(total)
            total = jnp.sum(sum(ordered(chips, at_query, side)))
            terms = terms - jnp.where(lane == done, total, 0.0)
            done += 1
    return terms


def put_terms(ref, terms):
    high = terms.astype(jnp.bfloat16)
    rest = terms - high.astype(jnp.float32)
    middle = rest.astype(jnp.bfloat16)
    low = (rest - middle.astype(jnp.float32)).astype(jnp.bfloat16)
    row = lax.broadcasted_iota(jnp.int32, (EXTRA, BLOCK), 0)
    rows = [part.astype(jnp.float32) for part in (high, middle, low)]
    block = jnp.zeros((EXTRA, BLOCK), jnp.float32)
    for place, part in enumerate(rows):
        block = jnp.where(row == place, part, block)
    ref[pl.ds(ref.shape[0] - EXTRA, EXTRA), :] = block.astype(jnp.bfloat16)


def get_terms(ref):
    block = ref[...].astype(jnp.float32)
    return block[0:1] + block[1:2] + block[2:3]


def grads_kernel(first, heads, slots, side, scaling, groups, tiles, sink_ref, *refs):
    stat_groups = [refs[2 * slots + i * side :][:side] for i in range(groups)]
    stat_refs = stat_groups[-1]
    rest = refs[2 * slots + groups * side :]
    remote = slots - CORES
    if first:
        done = rest[0].shape[0]
        rest[3][:done, :] = rest[0][...]
        rest = rest[1:]
    dq_home, dkv_home, core_out = rest[:3]
    dq_out, dkv_out = rest[3 : 3 + remote], rest[3 + remote : 3 + 2 * remote]
    q_all, g_all, k_all, v_all, rows, dkeys, dvalues, dquery = rest[-8:]
    query_side, key_side = (q_all, g_all), (k_all, v_all)
    spread([(first, heads)], slots, refs, query_side, key_side)
    dkeys[...] = jnp.zeros_like(dkeys)
    dvalues[...] = jnp.zeros_like(dvalues)
    dquery[...] = jnp.zeros_like(dquery)
    for head in range(heads):
        for slot in range(slots):
            log_norm, row_delta = settle(
                stat_rows(stat_refs, head, slot, slots), sink_ref[first + head]
            )
            rows[head * slots + slot, 0:1, :] = log_norm
            rows[head * slots + slot, 1:2, :] = row_delta

    def work(query, one, two, scores, dprobs):
        weights = jnp.exp(scores * scaling - rows[query, 0:1, :])
        probs = weights.astype(jnp.bfloat16)
        dscores = (weights * (dprobs - rows[query, 1:2, :])).astype(jnp.bfloat16)
        dquery[query] += dot(paired(k_all, one, two), dscores, TN)
        dkey = dot(dscores, q_all[query], NN)
        dvalue = dot(probs, g_all[query], NN)
        dkeys[one] += dkey[:BLOCK]
        dkeys[two] += dkey[BLOCK:]
        dvalues[one] += dvalue[:BLOCK]
        dvalues[two] += dvalue[BLOCK:]

    walk(tiles, query_side, key_side, work)
    tokens = dq_home.shape[1]
    parts = tokens // BLOCK
    for head in range(heads):
        for slot in range(slots):
            place = head * slots + slot
            total = dquery[place].T * scaling
            if slot == 0:
                dq_home[head] = total
            elif slot < CORES:
                core_out[pl.ds((first + head) * 3 * tokens, tokens), :] = total.astype(jnp.bfloat16)
            else:
                dq_out[slot - CORES][pl.ds(head * tokens, tokens), :] = total.astype(jnp.bfloat16)
            for part in range(parts):
                span = pl.ds(part * BLOCK, BLOCK)
                dkey = dkeys[place * parts + part] * scaling
                dvalue = dvalues[place * parts + part]
                if slot == 0:
                    dkv_home[head, 0, span, :] = dkey
                    dkv_home[head, 1, span, :] = dvalue
                    continue
                if slot < CORES:
                    ref, start = core_out, ((first + head) * 3 + 1) * tokens + part * BLOCK
                else:
                    ref, start = dkv_out[slot - CORES], head * 2 * tokens + part * BLOCK
                ref[pl.ds(start, BLOCK), :] = dkey.astype(jnp.bfloat16)
                ref[pl.ds(start + tokens, BLOCK), :] = dvalue.astype(jnp.bfloat16)
    if groups > 1:
        _, at_query, _ = coordinates(side)
        terms = sink_terms(stat_groups, slots, side, sink_ref, at_query)
        terms_out = rest[3 + 2 * remote]
        terms_out[...] = jnp.broadcast_to(terms, terms_out.shape)
        for ref in (core_out, *dkv_out):
            put_terms(ref, terms)


def grads(tiles, sink, qd, kv, partials, before, first, heads, scaling):
    slots, tokens = len(qd), qd[0].shape[2]
    side, groups = len(partials[0]), len(partials)
    extra = EXTRA if groups > 1 else 0
    remote = slots - CORES
    blocks = heads * slots * (tokens // BLOCK)
    low, high = jnp.bfloat16, jnp.float32
    befores = [] if before is None else [before]
    operands = qd + kv + [each for group in partials for each in group] + befores
    shapes = [
        ((heads, tokens, BLOCK), high),
        ((heads, 2, tokens, BLOCK), high),
        (((first + heads) * 3 * tokens + extra, BLOCK), low),
    ]
    shapes += [((heads * tokens, BLOCK), low)] * remote
    shapes += [((heads * 2 * tokens + extra, BLOCK), low)] * remote
    shapes += [((8, BLOCK), high)] * (groups > 1)
    return pl.pallas_call(
        lambda *refs: grads_kernel(first, heads, slots, side, scaling, groups, *refs),
        in_specs=[pl.BlockSpec(memory_space=pltpu.SMEM)] * 2 + whole(len(operands)),
        out_specs=whole(len(shapes)),
        out_shape=[jax.ShapeDtypeStruct(shape, kind) for shape, kind in shapes],
        scratch_shapes=tile_scratch(heads, slots, tokens)
        + [pltpu.VMEM((blocks, BLOCK, BLOCK), high)] * 2
        + [pltpu.VMEM((heads * slots, BLOCK, tokens), high)],
        compiler_params=pltpu.CompilerParams(vmem_limit_bytes=VMEM_BYTES),
        cost_estimate=pl.CostEstimate(
            flops=heads * 4 * 10**9, bytes_accessed=1, transcendentals=0
        ),
        name="gradients",
    )(tiles, sink, *operands)


def gate(arrays, after):
    count = len(arrays)
    return pl.pallas_call(
        lambda *refs: None,
        in_specs=[pl.BlockSpec(memory_space=pl.ANY)] * (count + len(after)),
        out_specs=[pl.BlockSpec(memory_space=pl.ANY)] * count,
        out_shape=[jax.ShapeDtypeStruct(each.shape, each.dtype) for each in arrays],
        input_output_aliases={place: place for place in range(count)},
        compiler_params=pltpu.CompilerParams(vmem_limit_bytes=FEW_BYTES),
        cost_estimate=SMALL,
        name="gate",
    )(*arrays, *after)


def close_kernel(sizes, side, half, from_core, *refs):
    per = 2 + 4 * (side - 1)
    outs = refs[per * len(sizes) :]
    core = lax.axis_index("ctx") % CORES
    first = 0
    for chunk, heads in enumerate(sizes):
        dq_home, dkv_home, *far = refs[per * chunk : per * (chunk + 1)]
        dq_far, dkv_far = far[: 2 * (side - 1)], far[2 * (side - 1) :]
        tokens = dq_home.shape[1]
        for head in range(heads):
            mine = pl.ds(pl.multiple_of(core * half + first, BLOCK), BLOCK)
            other = pl.ds(pl.multiple_of((1 - core) * half + first, BLOCK), BLOCK)
            for place, out in enumerate(outs):
                if place == 0:
                    parts = [dq_home[head]]
                    parts += [ref[pl.ds(head * tokens, tokens), :] for ref in dq_far]
                else:
                    span = pl.ds((head * 2 + place - 1) * tokens, tokens)
                    parts = [dkv_home[head, place - 1]] + [ref[span, :] for ref in dkv_far]
                parts = [part.astype(jnp.float32) for part in parts]
                span = pl.ds((first // BLOCK * 3 + place) * tokens, tokens)
                start = from_core[span, :].astype(jnp.float32)
                out[0, :, mine] = sum(parts[1::2], parts[0]).astype(jnp.bfloat16)
                out[0, :, other] = sum(parts[2::2], start).astype(jnp.bfloat16)
            first += BLOCK


def close(pieces, from_core, sizes, side, half, tokens):
    flat = [from_core] + [piece for chunk in pieces for piece in chunk]
    return pl.pallas_call(
        lambda *refs: close_kernel(sizes, side, half, *refs),
        in_specs=whole(len(flat)),
        out_specs=whole(3),
        out_shape=[jax.ShapeDtypeStruct((1, tokens, 2 * half), jnp.bfloat16)] * 3,
        compiler_params=pltpu.CompilerParams(vmem_limit_bytes=VMEM_BYTES),
        cost_estimate=SMALL,
        name="closing_sums",
    )(*flat)


def halved(value, by):
    if by & (by - 1) == 0:
        return value >> (by.bit_length() - 1), value & (by - 1)
    return lax.div(value, jnp.int32(by)), lax.rem(value, jnp.int32(by))


def lists_kernel(spans, half_heads, side, per_group, listed, groups, *refs):
    asked, outs, spots = refs[: 2 * side], refs[2 * side : -1], refs[-1]
    slots = side * CORES
    rest, core = halved(lax.axis_index("ctx"), CORES)
    row, col = halved(rest, side)

    def one_owner(owner, carry):
        rest, its_core = halved(owner, CORES)
        its_row, its_col = halved(rest, side)
        across = jnp.where(core == 0, its_col == col, its_row == row)
        along = jnp.where(core == 0, its_row - row, its_col - col)
        shift = jnp.where(along < 0, along + side, along)
        spot = (shift * CORES + jnp.where(its_core == core, 0, 1)) * per_group
        for part in range(per_group):
            spots[owner * per_group + part] = jnp.where(across, spot + part, -1)
        return carry

    lax.fori_loop(0, groups, one_owner, 0)
    for (first, heads), out in zip(spans, outs):

        def one_head(head, count, first=first, out=out):
            for slot in range(slots):
                query = head * slots + slot
                base = head * (slots * per_group)
                code = query
                for part in range(per_group // 2 if slot < CORES else 0):
                    left = base + slot * per_group + 2 * part
                    out[count] = query + (left << 8) + ((left + 2) << 16)
                    count = count + 1
                held = jnp.int32(0)
                blocks = asked[slot]
                for entry in range(listed):
                    spot = spots[blocks[core * half_heads + first + head, 0, entry]]
                    here = (spot >= 0).astype(jnp.int32)
                    place = base + spot
                    longer = jnp.where(held == 0, query + (place << 8), code + ((place + 1) << 16))
                    code = jnp.where(spot >= 0, longer, code)
                    out[count] = code
                    count = count + (here & held)
                    held = held ^ here
                count = count + held
            return count

        out[0] = lax.fori_loop(0, heads, one_head, jnp.int32(1)) - 1


def tile_lists(asked, spans, half_heads, side, per_group, groups):
    slots, listed = len(asked), asked[0].shape[2]
    assert half_heads * slots * per_group < 255
    most = slots * ((listed + 1) // 2) + CORES * (per_group // 2)
    return pl.pallas_call(
        lambda *refs: lists_kernel(spans, half_heads, side, per_group, listed, groups, *refs),
        in_specs=[pl.BlockSpec(memory_space=pltpu.SMEM)] * slots,
        out_specs=[pl.BlockSpec(memory_space=pltpu.SMEM)] * len(spans),
        out_shape=[jax.ShapeDtypeStruct((heads * most + 8,), jnp.int32) for _, heads in spans],
        scratch_shapes=[pltpu.SMEM((groups * per_group,), jnp.int32)],
        compiler_params=pltpu.CompilerParams(vmem_limit_bytes=FEW_BYTES),
        cost_estimate=SMALL,
        name="tile_lists",
    )(*asked)


def sink_kernel(half_heads, side, terms_ref, core_ref, *refs):
    *far, out = refs
    core, at_query, at_key = coordinates(side)
    mine = [terms_ref[0:1, :]] + [get_terms(ref) for ref in far[0::CORES]]
    other = [get_terms(core_ref)] + [get_terms(ref) for ref in far[1::CORES]]
    mine = sum(ordered(mine, at_key, side))
    other = sum(ordered(other, at_query, side))
    lane = lax.broadcasted_iota(jnp.int32, (1, BLOCK), 1)
    low = jnp.where(core == 0, mine, other)
    high = pltpu.roll(jnp.where(core == 0, other, mine), half_heads, 1)
    terms = jnp.where(lane < half_heads, low, high)
    row = lax.broadcasted_iota(jnp.int32, out.shape, 0)
    out[...] = jnp.where(row == lax.axis_index("dp"), terms, 0.0)


def sink_sum(terms, from_core, far, half_heads, side):
    arrays = [from_core, *far]
    last = [
        pl.BlockSpec((EXTRA, BLOCK), lambda i, end=array.shape[0] // EXTRA - 1: (end, 0))
        for array in arrays
    ]
    shape = (lax.axis_size("dp"), BLOCK)
    return pl.pallas_call(
        lambda *refs: sink_kernel(half_heads, side, *refs),
        grid=(1,),
        in_specs=[pl.BlockSpec((8, BLOCK), lambda i: (0, 0))] + last,
        out_specs=pl.BlockSpec(shape, lambda i: (0, 0)),
        out_shape=jax.ShapeDtypeStruct(shape, jnp.float32),
        compiler_params=pltpu.CompilerParams(vmem_limit_bytes=FEW_BYTES),
        cost_estimate=SMALL,
        name="sink_sum",
    )(terms, *arrays)


def sink_rounds():
    copies = lax.axis_size("dp")
    assert copies & (copies - 1) == 0
    rounds, step = [], 1
    while step < copies:
        radix = 4 if copies % (4 * step) == 0 else 2
        perms = [
            [(i, (i + part * step) % copies) for i in range(copies)] for part in range(1, radix)
        ]
        rounds.append(("dp", perms))
        step *= radix
    return rounds


def sink_round(held, axis, perms):
    return sum([lax.ppermute(held, axis, perm) for perm in perms], held)


def body(query_in, key_in, value_in, grad_out, key_blocks, sink_logits):
    groups = lax.axis_size("ctx")
    side = grid_side(groups)
    slots = side * CORES
    head_count = sink_logits.shape[0]
    tokens = query_in.shape[1]
    per_group = tokens // BLOCK
    assert key_blocks.shape[1] == 1 and query_in.shape[2] == head_count * BLOCK
    assert per_group % 2 == 0 and head_count % CORES == 0
    half_heads = head_count // 2
    half = half_heads * BLOCK
    scaling = 1.0 / math.sqrt(BLOCK)
    sizes = chunk_sizes(half_heads)
    starts = [sum(sizes[:i]) for i in range(len(sizes))]
    core = lax.axis_index("ctx") % CORES
    swap = gather_perm(groups, side, True, 0, 1)
    places = [(shift, cross) for shift in range(1, side) for cross in range(CORES)]
    remote = len(places)
    sink = jnp.where(core == 0, sink_logits[:half_heads], sink_logits[half_heads:])

    from_core = lax.ppermute(key_blocks, "ctx", swap)
    pair = jnp.concatenate([key_blocks, from_core], axis=1)
    asked = [key_blocks, from_core]
    for shift in range(1, side):
        came = lax.ppermute(pair, "ctx", gather_perm(groups, side, True, shift, 0))
        asked += [came[:, cross : cross + 1] for cross in range(CORES)]
    spans = list(zip(starts, sizes))
    tiles = tile_lists(asked, spans, half_heads, side, per_group, groups)

    fields = (query_in, grad_out, key_in, value_in)
    qds, kvs = [], []
    for first, heads in zip(starts, sizes):
        last = first + heads == half_heads
        packed = pack(fields, first, heads, half_heads if last else 0, half)
        if not last:
            fields, packed, pair = lax.optimization_barrier((fields, packed, pair))
        qd_own, kv_own, qd_oth, kv_oth = packed[:4]
        if last:
            from_core = lax.ppermute(packed[4], "ctx", swap)
            tiles, packed = lax.optimization_barrier((tiles, packed))
            qd_own, kv_own, qd_oth, kv_oth = packed[:4]
        qd, kv = [qd_own], [kv_own]
        for shift, cross in places:
            perm = gather_perm(groups, side, True, shift, cross)
            qd.append(lax.ppermute(qd_oth if cross else qd_own, "ctx", perm))
            perm = gather_perm(groups, side, False, shift, cross)
            kv.append(lax.ppermute(kv_oth if cross else kv_own, "ctx", perm))
        qds.append(qd)
        kvs.append(kv)
    for qd, kv in zip(qds, kvs):
        qd.insert(1, from_core)
        kv.insert(1, from_core)

    partials = []
    for chunk, (first, heads) in enumerate(spans):
        partial = stats(tiles[chunk], sink, qds[chunk], kvs[chunk], first, heads, scaling)
        came = [
            lax.ppermute(partial, "ctx", gather_perm(groups, side, True, shift, 0))
            for shift in range(1, side)
        ]
        partials.append([partial] + came)
    pieces, core_out = [], None
    for chunk, (first, heads) in enumerate(spans):
        last = chunk == len(spans) - 1
        results = grads(
            tiles[chunk],
            sink,
            qds[chunk],
            kvs[chunk],
            partials if last else partials[chunk : chunk + 1],
            core_out,
            first,
            heads,
            scaling,
        )
        core_out = results[2]
        if pieces:
            results = results[:2] + gate(results[2 : 3 + 2 * remote], pieces[-1][2:]) + results[-1:]
            core_out = results[2]
        dq_out, dkv_out = results[3 : 3 + remote], results[3 + remote : 3 + 2 * remote]
        back = [
            lax.ppermute(value, "ctx", return_perm(groups, side, along_query, shift, cross))
            for along_query, values in ((True, dq_out), (False, dkv_out))
            for value, (shift, cross) in zip(values, places)
        ]
        pieces.append(list(results[:2]) + back)
    from_core = lax.ppermute(core_out, "ctx", swap)
    held = sink_sum(results[-1], from_core, pieces[-1][2 + remote :], half_heads, side)
    for each in sink_rounds():
        held = sink_round(held, *each)
    grad_sink = jnp.sum(held, axis=0)[:head_count]
    grad_query, grad_key, grad_value = close(pieces, from_core, sizes, side, half, tokens)
    return (grad_query, grad_key, grad_value, grad_sink)


def solution(mesh):
    tokens = P("dp", "ctx", None)
    return jax.shard_map(
        body,
        mesh=mesh,
        in_specs=(tokens, tokens, tokens, tokens, P(None, "ctx", None), P()),
        out_specs=(tokens, tokens, tokens, P()),
        check_vma=False,
    )
```

```python
import math

import jax
import jax.numpy as jnp
from jax import lax
from jax.experimental import pallas as pl
from jax.experimental.pallas import tpu as pltpu
from jax.sharding import PartitionSpec as P

BLOCK = 128
CORES = 2
FAR = -1e30
VMEM_BYTES = 24 * 1024 * 1024
FEW_BYTES = 2 * 1024 * 1024
MOST_BYTES = 62 * 1024 * 1024
UNROLL = 5
EXTRA = 16
SMALL = pl.CostEstimate(flops=1, bytes_accessed=1, transcendentals=0)
NT = (((1,), (1,)), ((), ()))
NN = (((1,), (0,)), ((), ()))
TN = (((0,), (0,)), ((), ()))


def chunk_sizes(heads):
    return (heads - 1, 1) if heads > 1 else (1,)


def part_spans(sizes, part_sizes):
    where = [(chunk, offset) for chunk, size in enumerate(sizes) for offset in range(size)]
    parts, done = [], 0
    for count in part_sizes:
        spans = []
        for head in range(done, done + count):
            chunk, offset = where[head]
            if spans and spans[-1][0] == chunk:
                spans[-1] = spans[-1][:3] + (spans[-1][3] + 1,)
            else:
                spans.append((chunk, offset, head, 1))
        parts.append(spans)
        done += count
    return parts


def part_sizes(heads):
    first = (heads + 1) // 2
    return [size for size in (first, heads - first) if size]


def grid_side(groups):
    side = math.isqrt(groups // CORES)
    assert CORES * side * side == groups
    return side


def moved(index, side, along_query, shift, cross):
    core, col, row = index % CORES, index // CORES % side, index // (CORES * side)
    along_col = (core == 0) == along_query
    if along_col:
        col = (col + shift) % side
    else:
        row = (row + shift) % side
    return (row * side + col) * CORES + (core ^ cross)


def gather_perm(groups, side, along_query, shift, cross):
    return [(moved(i, side, along_query, shift, cross), i) for i in range(groups)]


def return_perm(groups, side, along_query, shift, cross):
    return [(i, moved(i, side, along_query, shift, cross)) for i in range(groups)]


def dot(lhs, rhs, dims):
    return lax.dot_general(lhs, rhs, dims, preferred_element_type=jnp.float32)


def whole(count):
    return [pl.BlockSpec(memory_space=pltpu.VMEM)] * count


def pack_kernel(blocks, half, q_ref, g_ref, k_ref, v_ref, *rest):
    outs, (held, came, left) = rest[:-3], rest[-3:]
    core = lax.axis_index("ctx") % CORES
    arriving, leaving = [], []
    for count, (which, head, field, _) in enumerate(blocks):
        start = (core if which == 0 else 1 - core) * half + head * BLOCK
        columns = pl.ds(pl.multiple_of(start, BLOCK), BLOCK)
        copy = pltpu.make_async_copy(
            (q_ref, g_ref, k_ref, v_ref)[field].at[0, :, columns], held.at[count], came.at[count]
        )
        copy.start()
        arriving.append(copy)
    for count, (copy, (*_, targets)) in enumerate(zip(arriving, blocks)):
        copy.wait()
        for out, row, place in targets:
            leaving.append(
                pltpu.make_async_copy(
                    held.at[count], outs[out].at[row, place], left.at[len(leaving)]
                )
            )
            leaving[-1].start()
    for copy in leaving:
        copy.wait()


def pack(fields, sizes, half):
    tokens = fields[0].shape[1]
    blocks, first = [], 0
    for chunk, heads in enumerate(sizes):
        for row in range(heads):
            for which in range(2):
                for field in range(4):
                    targets = [(4 * chunk + 2 * which + field // 2, row, field % 2)]
                    targets += [(4 * len(sizes), first + row, field)] * which
                    blocks.append((which, first + row, field, targets))
        first += heads
    shapes = [(size, 2, tokens, BLOCK) for size in sizes for _ in range(4)]
    shapes.append((first, 4, tokens, BLOCK))
    return pl.pallas_call(
        lambda *refs: pack_kernel(blocks, half, *refs),
        in_specs=[pl.BlockSpec(memory_space=pl.ANY)] * 4,
        out_specs=[pl.BlockSpec(memory_space=pl.ANY)] * len(shapes),
        out_shape=[jax.ShapeDtypeStruct(shape, jnp.bfloat16) for shape in shapes],
        scratch_shapes=[
            pltpu.VMEM((len(blocks), tokens, BLOCK), jnp.bfloat16),
            pltpu.SemaphoreType.DMA((len(blocks),)),
            pltpu.SemaphoreType.DMA((sum(len(block[-1]) for block in blocks),)),
        ],
        compiler_params=pltpu.CompilerParams(vmem_limit_bytes=MOST_BYTES),
        cost_estimate=pl.CostEstimate(flops=4 * 10**9, bytes_accessed=1, transcendentals=0),
        name="pack",
    )(*fields)


def spread(spans, slots, refs, query_side, key_side):
    place = 0
    for span, (_, offset, first, heads) in enumerate(spans):
        here = refs[span * 2 * slots : (span + 1) * 2 * slots]
        qd_refs, kv_refs = here[:slots], here[slots:]
        parts = kv_refs[0].shape[2] // BLOCK
        for head in range(heads):
            for slot in range(slots):
                from_core = slot == 1
                row = head + (first if from_core else offset)
                for kind in range(2):
                    lead = kind + (2 if from_core else 0)
                    query_side[kind][place] = qd_refs[slot][row, kind]
                    for part in range(parts):
                        key_side[kind][place * parts + part] = kv_refs[slot][
                            row, lead, pl.ds(part * BLOCK, BLOCK), :
                        ]
                place += 1


def paired(ref, one, two):
    return jnp.concatenate([ref[one], ref[two]], axis=0)


def tile_products(tile, tiles, query_side, key_side):
    bound = tiles[0]
    real = tile < bound
    code = tiles[1 + jnp.minimum(tile, bound - 1)]
    query, one, two = code & 255, (code >> 8) & 255, (code >> 16) - 1
    both = real & (two >= 0)
    two = jnp.maximum(two, 0)
    raw = dot(paired(key_side[0], one, two), query_side[0][query], NT)
    scores = jnp.concatenate(
        [raw[:BLOCK] + jnp.where(real, 0.0, FAR), raw[BLOCK:] + jnp.where(both, 0.0, FAR)], axis=0
    )
    dprobs = dot(paired(key_side[1], one, two), query_side[1][query], NT)
    return query, one, two, scores, dprobs


def walk(tiles, query_side, key_side, work):
    def step(index, carry):
        made = [
            tile_products(UNROLL * index + i, tiles, query_side, key_side) for i in range(UNROLL)
        ]
        for one in made:
            work(*one)
        return carry

    lax.fori_loop(0, (tiles[0] + UNROLL - 1) // UNROLL, step, 0)


def tile_scratch(heads, slots, tokens):
    query_side = pltpu.VMEM((heads * slots, tokens, BLOCK), jnp.bfloat16)
    key_side = pltpu.VMEM((heads * slots * (tokens // BLOCK), BLOCK, BLOCK), jnp.bfloat16)
    return [query_side] * 2 + [key_side] * 2 + [pltpu.VMEM((heads * slots, 8, tokens), jnp.float32)]


def stats_kernel(first, heads, slots, scaling, tiles, sink_ref, *refs):
    out_ref, q_all, g_all, k_all, v_all, rows = refs[-6:]
    query_side, key_side = (q_all, g_all), (k_all, v_all)
    spread([(0, 0, first, heads)], slots, refs, query_side, key_side)
    zero = jnp.zeros((1, out_ref.shape[2]), jnp.float32)
    for head in range(heads):
        for slot in range(slots):
            rows[head * slots + slot, 0:1, :] = zero + sink_ref[first + head]
            rows[head * slots + slot, 1:2, :] = zero
            rows[head * slots + slot, 2:3, :] = zero

    def work(query, one, two, scores, dprobs):
        old = rows[query, 0:1, :]
        top = jnp.maximum(old, jnp.max(scores, axis=0, keepdims=True) * scaling)
        parts = jnp.exp(scores * scaling - top)
        shrink = jnp.exp(old - top)
        rows[query, 0:1, :] = top
        rows[query, 1:2, :] = rows[query, 1:2, :] * shrink + jnp.sum(parts, axis=0, keepdims=True)
        rows[query, 2:3, :] = rows[query, 2:3, :] * shrink + jnp.sum(
            parts * dprobs, axis=0, keepdims=True
        )

    walk(tiles, query_side, key_side, work)
    for head in range(heads):
        for slot in range(slots):
            for kind in range(3):
                out_ref[head, pl.ds(kind * slots + slot, 1), :] = rows[
                    head * slots + slot, kind : kind + 1, :
                ]


def stats(tiles, sink, qd, kv, first, heads, scaling):
    slots, tokens = len(qd), qd[0].shape[2]
    rows = -(-3 * slots // 8) * 8
    return pl.pallas_call(
        lambda *refs: stats_kernel(first, heads, slots, scaling, *refs),
        in_specs=[pl.BlockSpec(memory_space=pltpu.SMEM)] * 2 + whole(2 * slots),
        out_specs=whole(1)[0],
        out_shape=jax.ShapeDtypeStruct((heads, rows, tokens), jnp.float32),
        scratch_shapes=tile_scratch(heads, slots, tokens),
        compiler_params=pltpu.CompilerParams(vmem_limit_bytes=VMEM_BYTES),
        cost_estimate=SMALL,
        name="row_stats",
    )(tiles, sink, *qd, *kv)


def settle(parts, sink):
    top = parts[0][0]
    for part in parts[1:]:
        top = jnp.maximum(top, part[0])
    total, mixed = jnp.exp(sink - top), jnp.zeros_like(top)
    for part in parts:
        grow = jnp.exp(part[0] - top)
        total = total + part[1] * grow
        mixed = mixed + part[2] * grow
    return top + jnp.log(total), mixed / total


def stat_place(slot, shift, side):
    return (slot // CORES - shift) % side * CORES + slot % CORES


def stat_rows(refs, head, slot, slots):
    side = len(refs)
    return [
        [ref[head, pl.ds(kind * slots + stat_place(slot, shift, side), 1), :] for kind in range(3)]
        for shift, ref in enumerate(refs)
    ]


def ordered(items, at, side):
    made = []
    for place in range(side):
        value = items[place]
        for own in range(1, side):
            value = jnp.where(at == own, items[(place - own) % side], value)
        made.append(value)
    return made


def coordinates(side):
    rest, core = halved(lax.axis_index("ctx"), CORES)
    row, col = halved(rest, side)
    return core, jnp.where(core == 0, col, row), jnp.where(core == 0, row, col)


def put_terms(ref, terms):
    high = terms.astype(jnp.bfloat16)
    rest = terms - high.astype(jnp.float32)
    middle = rest.astype(jnp.bfloat16)
    low = (rest - middle.astype(jnp.float32)).astype(jnp.bfloat16)
    row = lax.broadcasted_iota(jnp.int32, (EXTRA, BLOCK), 0)
    rows = [part.astype(jnp.float32) for part in (high, middle, low)]
    block = jnp.zeros((EXTRA, BLOCK), jnp.float32)
    for place, part in enumerate(rows):
        block = jnp.where(row == place, part, block)
    ref[...] = block.astype(jnp.bfloat16)


def get_terms(ref):
    block = ref[pl.ds(ref.shape[0] - EXTRA, EXTRA), :].astype(jnp.float32)
    return block[0:1] + block[1:2] + block[2:3]


def grads_kernel(spans, slots, side, scaling, lead, joins, tiles, sink_ref, *refs):
    first, heads = spans[0][2], sum(span[-1] for span in spans)
    per_span = 2 * slots + side
    rest = refs[per_span * len(spans) :]
    remote = slots - CORES
    outs = rest[-11 - 2 * remote : -8]
    for before, place in zip(rest, joins):
        outs[place][: before.shape[0]] = before[...]
    dq_home, dkv_home, core_out = outs[:3]
    dq_out, dkv_out = outs[3 : 3 + remote], outs[3 + remote :]
    q_all, g_all, k_all, v_all, rows, dkeys, dvalues, dquery = rest[-8:]
    query_side, key_side = (q_all, g_all), (k_all, v_all)
    spread(spans, slots, refs, query_side, key_side)
    dkeys[...] = jnp.zeros_like(dkeys)
    dvalues[...] = jnp.zeros_like(dvalues)
    dquery[...] = jnp.zeros_like(dquery)
    place = 0
    for span, (_, offset, start, count) in enumerate(spans):
        stat_refs = refs[2 * slots * len(spans) + side * span :][:side]
        for head in range(count):
            for slot in range(slots):
                log_norm, row_delta = settle(
                    stat_rows(stat_refs, offset + head, slot, slots), sink_ref[start + head]
                )
                rows[place, 0:1, :] = log_norm
                rows[place, 1:2, :] = row_delta
                place += 1

    def work(query, one, two, scores, dprobs):
        weights = jnp.exp(scores * scaling - rows[query, 0:1, :])
        probs = weights.astype(jnp.bfloat16)
        dscores = (weights * (dprobs - rows[query, 1:2, :])).astype(jnp.bfloat16)
        dquery[query] += dot(paired(k_all, one, two), dscores, TN)
        dkey = dot(dscores, q_all[query], NN)
        dvalue = dot(probs, g_all[query], NN)
        dkeys[one] += dkey[:BLOCK]
        dkeys[two] += dkey[BLOCK:]
        dvalues[one] += dvalue[:BLOCK]
        dvalues[two] += dvalue[BLOCK:]

    walk(tiles, query_side, key_side, work)
    tokens = dq_home.shape[1]
    parts = tokens // BLOCK
    for head in range(heads):
        for slot in range(slots):
            place = head * slots + slot
            total = dquery[place].T * scaling
            if slot == 0:
                dq_home[lead + head] = total
            elif slot < CORES:
                core_out[pl.ds((first + head) * 3 * tokens, tokens), :] = total.astype(jnp.bfloat16)
            else:
                dq_out[slot - CORES][pl.ds((lead + head) * tokens, tokens), :] = total.astype(jnp.bfloat16)
            for part in range(parts):
                span = pl.ds(part * BLOCK, BLOCK)
                dkey = dkeys[place * parts + part] * scaling
                dvalue = dvalues[place * parts + part]
                if slot == 0:
                    dkv_home[lead + head, 0, span, :] = dkey
                    dkv_home[lead + head, 1, span, :] = dvalue
                    continue
                if slot < CORES:
                    ref, start = core_out, ((first + head) * 3 + 1) * tokens + part * BLOCK
                else:
                    ref, start = dkv_out[slot - CORES], (lead + head) * 2 * tokens + part * BLOCK
                ref[pl.ds(start, BLOCK), :] = dkey.astype(jnp.bfloat16)
                ref[pl.ds(start + tokens, BLOCK), :] = dvalue.astype(jnp.bfloat16)


def grads(tiles, sink, qds, kvs, partials, before, join, after, spans, last, scaling):
    slots, tokens = len(qds[0]), qds[0][0].shape[2]
    first, heads = spans[0][2], sum(span[-1] for span in spans)
    side = len(partials[0])
    extra = EXTRA if last else 0
    remote = slots - CORES
    blocks = heads * slots * (tokens // BLOCK)
    low, high = jnp.bfloat16, jnp.float32
    joins = [] if before is None else list(range(len(before))) if join else [2]
    lead = before[0].shape[0] if join else 0
    count = lead + heads
    operands = [each for chunk, *_ in spans for each in qds[chunk] + kvs[chunk]]
    operands += [each for chunk, *_ in spans for each in partials[chunk]]
    operands += [before[place] for place in joins]
    shapes = [
        ((count, tokens, BLOCK), high),
        ((count, 2, tokens, BLOCK), high),
        (((first + heads) * 3 * tokens + extra, BLOCK), low),
    ]
    shapes += [((count * tokens, BLOCK), low)] * remote
    shapes += [((count * 2 * tokens + extra, BLOCK), low)] * remote
    return pl.pallas_call(
        lambda *refs: grads_kernel(spans, slots, side, scaling, lead, joins, *refs),
        in_specs=[pl.BlockSpec(memory_space=pltpu.SMEM)] * 2
        + whole(len(operands))
        + [pl.BlockSpec(memory_space=pl.ANY)] * len(after),
        out_specs=whole(len(shapes)),
        out_shape=[jax.ShapeDtypeStruct(shape, kind) for shape, kind in shapes],
        scratch_shapes=tile_scratch(heads, slots, tokens)
        + [pltpu.VMEM((blocks, BLOCK, BLOCK), high)] * 2
        + [pltpu.VMEM((heads * slots, BLOCK, tokens), high)],
        compiler_params=pltpu.CompilerParams(vmem_limit_bytes=VMEM_BYTES),
        cost_estimate=pl.CostEstimate(
            flops=heads * 4 * 10**9, bytes_accessed=1, transcendentals=0
        ),
        name="gradients",
    )(tiles, sink, *operands, *after)


def gate(arrays, after):
    count = len(arrays)
    return pl.pallas_call(
        lambda *refs: None,
        in_specs=[pl.BlockSpec(memory_space=pl.ANY)] * (count + len(after)),
        out_specs=[pl.BlockSpec(memory_space=pl.ANY)] * count,
        out_shape=[jax.ShapeDtypeStruct(each.shape, each.dtype) for each in arrays],
        input_output_aliases={place: place for place in range(count)},
        compiler_params=pltpu.CompilerParams(vmem_limit_bytes=FEW_BYTES),
        cost_estimate=SMALL,
        name="gate",
    )(*arrays, *after)


def close_kernel(sizes, side, half, sums_ref, from_core, *refs):
    per = 2 + 4 * (side - 1)
    *outs, sink_out = refs[per * len(sizes) :]
    core = lax.axis_index("ctx") % CORES
    first = 0
    for chunk, heads in enumerate(sizes):
        dq_home, dkv_home, *far = refs[per * chunk : per * (chunk + 1)]
        dq_far, dkv_far = far[: 2 * (side - 1)], far[2 * (side - 1) :]
        tokens = dq_home.shape[1]
        for head in range(heads):
            mine = pl.ds(pl.multiple_of(core * half + first, BLOCK), BLOCK)
            other = pl.ds(pl.multiple_of((1 - core) * half + first, BLOCK), BLOCK)
            for place, out in enumerate(outs):
                if place == 0:
                    parts = [dq_home[head]]
                    parts += [ref[pl.ds(head * tokens, tokens), :] for ref in dq_far]
                else:
                    span = pl.ds((head * 2 + place - 1) * tokens, tokens)
                    parts = [dkv_home[head, place - 1]] + [ref[span, :] for ref in dkv_far]
                parts = [part.astype(jnp.float32) for part in parts]
                span = pl.ds((first // BLOCK * 3 + place) * tokens, tokens)
                start = from_core[span, :].astype(jnp.float32)
                out[0, :, mine] = sum(parts[1::2], parts[0]).astype(jnp.bfloat16)
                out[0, :, other] = sum(parts[2::2], start).astype(jnp.bfloat16)
            first += BLOCK
    half_heads = half // BLOCK
    _, at_query, at_key = coordinates(side)
    far = refs[per * len(sizes) - 2 * (side - 1) : per * len(sizes)]
    mine = [sums_ref[0:1, :]] + [get_terms(ref) for ref in far[0::2]]
    other = [get_terms(from_core)] + [get_terms(ref) for ref in far[1::2]]
    mine, other = sum(ordered(mine, at_key, side)), sum(ordered(other, at_query, side))
    low = jnp.where(core == 0, mine, other)
    high = pltpu.roll(jnp.where(core == 0, other, mine), half_heads, 1)
    lane = lax.broadcasted_iota(jnp.int32, (1, BLOCK), 1)
    sink_out[...] = jnp.where(lane < half_heads, low, high)[:, : 2 * half_heads]


def close(pieces, from_core, sums, sizes, side, half, tokens):
    flat = [sums, from_core] + [piece for chunk in pieces for piece in chunk]
    return pl.pallas_call(
        lambda *refs: close_kernel(sizes, side, half, *refs),
        in_specs=whole(len(flat)),
        out_specs=whole(4),
        out_shape=[jax.ShapeDtypeStruct((1, tokens, 2 * half), jnp.bfloat16)] * 3
        + [jax.ShapeDtypeStruct((1, 2 * half // BLOCK), jnp.float32)],
        compiler_params=pltpu.CompilerParams(vmem_limit_bytes=VMEM_BYTES),
        cost_estimate=SMALL,
        name="closing_sums",
    )(*flat)


def halved(value, by):
    if by & (by - 1) == 0:
        return value >> (by.bit_length() - 1), value & (by - 1)
    return lax.div(value, jnp.int32(by)), lax.rem(value, jnp.int32(by))


def lists_kernel(spans, half_heads, side, per_group, listed, groups, *refs):
    slots = side * CORES
    asked, refs = refs[:slots], refs[slots:]
    own = (len(refs) - 2 - len(spans)) // 2
    outs, stages, spots, sems = refs[own : own + len(spans)], refs[own + len(spans) : -2], refs[-2], refs[-1]
    copies = [
        pltpu.make_async_copy(source, stage, sems.at[place])
        for place, (source, stage) in enumerate(zip(refs, stages))
    ]
    for copy in copies:
        copy.start()
    rest, core = halved(lax.axis_index("ctx"), CORES)
    row, col = halved(rest, side)

    def one_owner(owner, carry):
        rest, its_core = halved(owner, CORES)
        its_row, its_col = halved(rest, side)
        across = jnp.where(core == 0, its_col == col, its_row == row)
        along = jnp.where(core == 0, its_row - row, its_col - col)
        shift = jnp.where(along < 0, along + side, along)
        spot = (shift * CORES + jnp.where(its_core == core, 0, 1)) * per_group
        for part in range(per_group):
            spots[owner * per_group + part] = jnp.where(across, spot + part, -1)
        return carry

    lax.fori_loop(0, groups, one_owner, 0)
    for (first, heads), out in zip(spans, outs):

        def one_head(head, count, first=first, out=out):
            for slot in range(slots):
                query = head * slots + slot
                base = head * (slots * per_group)
                code = query
                for part in range(per_group // 2 if slot < CORES else 0):
                    left = base + slot * per_group + 2 * part
                    out[count] = query + (left << 8) + ((left + 2) << 16)
                    count = count + 1
                held = jnp.int32(0)
                blocks = asked[slot]
                for entry in range(listed):
                    spot = spots[blocks[core * half_heads + first + head, 0, entry]]
                    here = (spot >= 0).astype(jnp.int32)
                    place = base + spot
                    longer = jnp.where(held == 0, query + (place << 8), code + ((place + 1) << 16))
                    code = jnp.where(spot >= 0, longer, code)
                    out[count] = code
                    count = count + (here & held)
                    held = held ^ here
                count = count + held
            return count

        out[0] = lax.fori_loop(0, heads, one_head, jnp.int32(1)) - 1
    for copy in copies:
        copy.wait()


def tile_lists(asked, own, spans, half_heads, side, per_group, groups):
    slots, listed = len(asked), asked[0].shape[2]
    assert half_heads * slots * per_group < 255
    most = slots * ((listed + 1) // 2) + CORES * (per_group // 2)
    return pl.pallas_call(
        lambda *refs: lists_kernel(spans, half_heads, side, per_group, listed, groups, *refs),
        in_specs=[pl.BlockSpec(memory_space=pltpu.SMEM)] * slots
        + [pl.BlockSpec(memory_space=pl.ANY)] * len(own),
        out_specs=[pl.BlockSpec(memory_space=pltpu.SMEM)] * len(spans) + whole(len(own)),
        out_shape=[jax.ShapeDtypeStruct((heads * most + 8,), jnp.int32) for _, heads in spans]
        + [jax.ShapeDtypeStruct(each.shape, each.dtype) for each in own],
        scratch_shapes=[
            pltpu.SMEM((groups * per_group,), jnp.int32),
            pltpu.SemaphoreType.DMA((len(own),)),
        ],
        compiler_params=pltpu.CompilerParams(vmem_limit_bytes=VMEM_BYTES),
        cost_estimate=SMALL,
        name="tile_lists",
    )(*asked, *own)


def sink_kernel(sizes, slots, side, sink_ref, *refs):
    out = refs[-1]
    _, at_query, _ = coordinates(side)
    lane = lax.broadcasted_iota(jnp.int32, (1, BLOCK), 1)
    terms = jnp.zeros((1, BLOCK), jnp.float32)
    done = 0
    for chunk, heads in enumerate(sizes):
        stat_refs = refs[chunk * side : (chunk + 1) * side]
        for head in range(heads):
            sink = sink_ref[done]
            chips = []
            for shift in range(side):
                total = 0.0
                for cross in range(CORES):
                    rows = stat_rows(stat_refs, head, shift * CORES + cross, slots)
                    kinds = [ordered(kind, at_query, side) for kind in zip(*rows)]
                    log_norm, row_delta = settle(list(zip(*kinds)), sink)
                    total = total + jnp.exp(sink - log_norm) * row_delta
                chips.append(total)
            total = jnp.sum(sum(ordered(chips, at_query, side)))
            terms = terms - jnp.where(lane == done, total, 0.0)
            done += 1
    row = lax.broadcasted_iota(jnp.int32, out.shape, 0)
    out[...] = jnp.where(row == lax.axis_index("dp"), terms, 0.0)


def sink_terms(partials, sink, sizes, slots, side, after):
    operands = [part for parts in partials for part in parts]
    return pl.pallas_call(
        lambda *refs: sink_kernel(sizes, slots, side, *refs),
        in_specs=[pl.BlockSpec(memory_space=pltpu.SMEM)]
        + whole(len(operands))
        + [pl.BlockSpec(memory_space=pl.ANY)] * len(after),
        out_specs=whole(1)[0],
        out_shape=jax.ShapeDtypeStruct((lax.axis_size("dp"), BLOCK), jnp.float32),
        compiler_params=pltpu.CompilerParams(vmem_limit_bytes=FEW_BYTES),
        cost_estimate=SMALL,
        name="sink_terms",
    )(sink, *operands, *after)


def sink_mark(held, messages, arrays, after):
    count = len(messages)

    def kernel(held_ref, *refs):
        total = jnp.sum(held_ref[...], axis=0, keepdims=True)
        sum_ref, *outs = refs[count + len(arrays) + len(after) :]
        sum_ref[...] = jnp.broadcast_to(total, sum_ref.shape)
        for out in outs[:count]:
            put_terms(out, total)

    any_spec = pl.BlockSpec(memory_space=pl.ANY)
    ends = [
        pl.BlockSpec((EXTRA, BLOCK), lambda i, end=each.shape[0] // EXTRA - 1: (end, 0))
        for each in messages
    ]
    passed = [*messages, *arrays]
    return pl.pallas_call(
        kernel,
        grid=(1,),
        in_specs=[pl.BlockSpec(held.shape, lambda i: (0, 0))]
        + [any_spec] * (len(passed) + len(after)),
        out_specs=[pl.BlockSpec((8, BLOCK), lambda i: (0, 0))] + ends + [any_spec] * len(arrays),
        out_shape=[jax.ShapeDtypeStruct((8, BLOCK), jnp.float32)]
        + [jax.ShapeDtypeStruct(each.shape, each.dtype) for each in passed],
        input_output_aliases={place + 1: place + 1 for place in range(len(passed))},
        compiler_params=pltpu.CompilerParams(vmem_limit_bytes=FEW_BYTES),
        cost_estimate=SMALL,
        name="sink_mark",
    )(held, *passed, *after)


def sink_rounds():
    copies = lax.axis_size("dp")
    assert copies & (copies - 1) == 0
    steps = [1 << bit for bit in range(copies.bit_length() - 1)]
    return [("dp", [[(i, (i + step) % copies) for i in range(copies)]]) for step in steps]


def sink_round(held, axis, perms):
    return sum([lax.ppermute(held, axis, perm) for perm in perms], held)


def body(query_in, key_in, value_in, grad_out, key_blocks, sink_logits):
    groups = lax.axis_size("ctx")
    side = grid_side(groups)
    slots = side * CORES
    head_count = sink_logits.shape[0]
    tokens = query_in.shape[1]
    per_group = tokens // BLOCK
    assert key_blocks.shape[1] == 1 and query_in.shape[2] == head_count * BLOCK
    assert per_group % 2 == 0 and head_count % CORES == 0
    half_heads = head_count // 2
    half = half_heads * BLOCK
    scaling = 1.0 / math.sqrt(BLOCK)
    sizes = chunk_sizes(half_heads)
    starts = [sum(sizes[:i]) for i in range(len(sizes))]
    core = lax.axis_index("ctx") % CORES
    swap = gather_perm(groups, side, True, 0, 1)
    places = [(shift, cross) for shift in range(1, side) for cross in range(CORES)]
    remote = len(places)
    sink = jnp.where(core == 0, sink_logits[:half_heads], sink_logits[half_heads:])

    from_core = lax.ppermute(key_blocks, "ctx", swap)
    pair = jnp.concatenate([key_blocks, from_core], axis=1)
    asked = [key_blocks, from_core]
    for shift in range(1, side):
        came = lax.ppermute(pair, "ctx", gather_perm(groups, side, True, shift, 0))
        asked += [came[:, cross : cross + 1] for cross in range(CORES)]
    spans = list(zip(starts, sizes))
    parts = part_spans(sizes, part_sizes(half_heads))
    part_heads = [(part[0][2], sum(span[-1] for span in part)) for part in parts]
    fields = (query_in, grad_out, key_in, value_in)
    packed = pack(fields, sizes, half)
    own = [packed[4 * chunk + pair] for chunk in range(len(sizes)) for pair in range(2)]
    made = tile_lists(asked, own, spans + part_heads, half_heads, side, per_group, groups)
    tiles, own = made[: len(spans) + len(parts)], made[len(spans) + len(parts) :]
    from_core = lax.ppermute(packed[-1], "ctx", swap)
    qds, kvs = [], []
    for chunk in range(len(sizes)):
        here = packed[4 * chunk : 4 * chunk + 4]
        if chunk:
            here = gate(here, [*tiles, from_core])
        qd_own, kv_own, qd_oth, kv_oth = here
        qd, kv = [own[2 * chunk]], [own[2 * chunk + 1]]
        for shift, cross in places:
            perm = gather_perm(groups, side, True, shift, cross)
            qd.append(lax.ppermute(qd_oth if cross else qd_own, "ctx", perm))
            perm = gather_perm(groups, side, False, shift, cross)
            kv.append(lax.ppermute(kv_oth if cross else kv_own, "ctx", perm))
        qds.append(qd)
        kvs.append(kv)
    for qd, kv in zip(qds, kvs):
        qd.insert(1, from_core)
        kv.insert(1, from_core)

    partials = []
    for chunk, (first, heads) in enumerate(spans):
        partial = stats(tiles[chunk], sink, qds[chunk], kvs[chunk], first, heads, scaling)
        came = [
            lax.ppermute(partial, "ctx", gather_perm(groups, side, True, shift, 0))
            for shift in range(1, side)
        ]
        partials.append([partial] + came)
    rounds = sink_rounds()
    results, pieces, after = None, [], []
    for number, part in enumerate(parts):
        last = number == len(parts) - 1
        if number == 1 or last and not pieces:
            held = sink_terms(partials, sink, sizes, slots, side, [] if last else results[:1])
        if number >= 1 and rounds:
            after = [held]
            held = sink_round(held, *rounds.pop(0))
        results = grads(
            tiles[len(spans) + number],
            sink,
            qds,
            kvs,
            partials,
            results,
            number >= 2,
            after,
            part,
            last,
            scaling,
        )
        if number >= 1 and not last:
            continue
        sent = results[3:]
        if last:
            for each in rounds:
                held = sink_round(held, *each)
            arriving = pieces[-1][2:] if pieces else []
            sums, core_out, *sent = sink_mark(
                held, [results[2], *sent[remote:]], sent[:remote], arriving
            )
            sent = sent[remote:] + sent[:remote]
        back = [
            lax.ppermute(value, "ctx", return_perm(groups, side, along_query, shift, cross))
            for along_query, values in ((True, sent[:remote]), (False, sent[remote:]))
            for value, (shift, cross) in zip(values, places)
        ]
        pieces.append(list(results[:2]) + back)
    from_core = lax.ppermute(core_out, "ctx", swap)
    sent_sizes = [part_sizes(half_heads)[0], half_heads - part_sizes(half_heads)[0]]
    grad_query, grad_key, grad_value, sinks = close(
        pieces, from_core, sums, [size for size in sent_sizes if size], side, half, tokens
    )
    grad_sink = sinks.reshape(head_count)
    return (grad_query, grad_key, grad_value, grad_sink)


def solution(mesh):
    tokens = P("dp", "ctx", None)
    return jax.shard_map(
        body,
        mesh=mesh,
        in_specs=(tokens, tokens, tokens, tokens, P(None, "ctx", None), P()),
        out_specs=(tokens, tokens, tokens, P()),
        check_vma=False,
    )
```

```python
import math

import jax
import jax.numpy as jnp
from jax import lax
from jax.experimental import pallas as pl
from jax.experimental.pallas import tpu as pltpu
from jax.sharding import PartitionSpec as P

BLOCK = 128
CORES = 2
FAR = -1e30
VMEM_BYTES = 24 * 1024 * 1024
FEW_BYTES = 2 * 1024 * 1024
MOST_BYTES = 62 * 1024 * 1024
MANY, FEW = 10, 5
EXTRA = 16
SMALL = pl.CostEstimate(flops=1, bytes_accessed=1, transcendentals=0)
NT = (((1,), (1,)), ((), ()))
NN = (((1,), (0,)), ((), ()))
TN = (((0,), (0,)), ((), ()))


def chunk_sizes(heads):
    return (heads - 1, 1) if heads > 1 else (1,)


def part_spans(sizes, part_sizes):
    where = [(chunk, offset) for chunk, size in enumerate(sizes) for offset in range(size)]
    parts, done = [], 0
    for count in part_sizes:
        spans = []
        for head in range(done, done + count):
            chunk, offset = where[head]
            if spans and spans[-1][0] == chunk:
                spans[-1] = spans[-1][:3] + (spans[-1][3] + 1,)
            else:
                spans.append((chunk, offset, head, 1))
        parts.append(spans)
        done += count
    return parts


def part_sizes(heads):
    first = (heads + 1) // 2
    return [size for size in (first, heads - first) if size]


def grid_side(groups):
    side = math.isqrt(groups // CORES)
    assert CORES * side * side == groups
    return side


def moved(index, side, along_query, shift, cross):
    core, col, row = index % CORES, index // CORES % side, index // (CORES * side)
    along_col = (core == 0) == along_query
    if along_col:
        col = (col + shift) % side
    else:
        row = (row + shift) % side
    return (row * side + col) * CORES + (core ^ cross)


def gather_perm(groups, side, along_query, shift, cross):
    return [(moved(i, side, along_query, shift, cross), i) for i in range(groups)]


def return_perm(groups, side, along_query, shift, cross):
    return [(i, moved(i, side, along_query, shift, cross)) for i in range(groups)]


def dot(lhs, rhs, dims):
    return lax.dot_general(lhs, rhs, dims, preferred_element_type=jnp.float32)


def whole(count):
    return [pl.BlockSpec(memory_space=pltpu.VMEM)] * count


def pack_kernel(blocks, half, q_ref, g_ref, k_ref, v_ref, *rest):
    outs, (held, came, left) = rest[:-3], rest[-3:]
    core = lax.axis_index("ctx") % CORES
    arriving, leaving = [], []
    for count, (which, head, field, _) in enumerate(blocks):
        start = (core if which == 0 else 1 - core) * half + head * BLOCK
        columns = pl.ds(pl.multiple_of(start, BLOCK), BLOCK)
        copy = pltpu.make_async_copy(
            (q_ref, g_ref, k_ref, v_ref)[field].at[0, :, columns], held.at[count], came.at[count]
        )
        copy.start()
        arriving.append(copy)
    for count, (copy, (*_, targets)) in enumerate(zip(arriving, blocks)):
        copy.wait()
        for out, row, place in targets:
            leaving.append(
                pltpu.make_async_copy(
                    held.at[count], outs[out].at[row, place], left.at[len(leaving)]
                )
            )
            leaving[-1].start()
    for copy in leaving:
        copy.wait()


def pack(fields, sizes, half):
    tokens = fields[0].shape[1]
    blocks, first = [], 0
    for chunk, heads in enumerate(sizes):
        for row in range(heads):
            for which in range(2):
                for field in range(4):
                    targets = [(4 * chunk + 2 * which + field // 2, row, field % 2)]
                    targets += [(4 * len(sizes), first + row, field)] * which
                    blocks.append((which, first + row, field, targets))
        first += heads
    shapes = [(size, 2, tokens, BLOCK) for size in sizes for _ in range(4)]
    shapes.append((first, 4, tokens, BLOCK))
    return pl.pallas_call(
        lambda *refs: pack_kernel(blocks, half, *refs),
        in_specs=[pl.BlockSpec(memory_space=pl.ANY)] * 4,
        out_specs=[pl.BlockSpec(memory_space=pl.ANY)] * len(shapes),
        out_shape=[jax.ShapeDtypeStruct(shape, jnp.bfloat16) for shape in shapes],
        scratch_shapes=[
            pltpu.VMEM((len(blocks), tokens, BLOCK), jnp.bfloat16),
            pltpu.SemaphoreType.DMA((len(blocks),)),
            pltpu.SemaphoreType.DMA((sum(len(block[-1]) for block in blocks),)),
        ],
        compiler_params=pltpu.CompilerParams(vmem_limit_bytes=MOST_BYTES),
        cost_estimate=pl.CostEstimate(flops=4 * 10**9, bytes_accessed=1, transcendentals=0),
        name="pack",
    )(*fields)


def spread(spans, slots, refs, query_side, key_side):
    place = 0
    for span, (_, offset, first, heads) in enumerate(spans):
        here = refs[span * 2 * slots : (span + 1) * 2 * slots]
        qd_refs, kv_refs = here[:slots], here[slots:]
        parts = kv_refs[0].shape[2] // BLOCK
        for head in range(heads):
            for slot in range(slots):
                from_core = slot == 1
                row = head + (first if from_core else offset)
                for kind in range(2):
                    lead = kind + (2 if from_core else 0)
                    query_side[kind][place] = qd_refs[slot][row, kind]
                    for part in range(parts):
                        key_side[kind][place * parts + part] = kv_refs[slot][
                            row, lead, pl.ds(part * BLOCK, BLOCK), :
                        ]
                place += 1


def paired(ref, one, two):
    return jnp.concatenate([ref[one], ref[two]], axis=0)


def tile_products(tile, tiles, query_side, key_side):
    bound = tiles[0]
    real = tile < bound
    code = tiles[1 + jnp.minimum(tile, bound - 1)]
    query, one, two = code & 255, (code >> 8) & 255, (code >> 16) - 1
    both = real & (two >= 0)
    two = jnp.maximum(two, 0)
    raw = dot(paired(key_side[0], one, two), query_side[0][query], NT)
    scores = jnp.concatenate(
        [raw[:BLOCK] + jnp.where(real, 0.0, FAR), raw[BLOCK:] + jnp.where(both, 0.0, FAR)], axis=0
    )
    dprobs = dot(paired(key_side[1], one, two), query_side[1][query], NT)
    return query, one, two, scores, dprobs


def walk(tiles, query_side, key_side, work):
    def steps(start, size, count):
        def step(index, carry):
            made = [
                tile_products(start + size * index + i, tiles, query_side, key_side)
                for i in range(size)
            ]
            for one in made:
                work(*one)
            return carry

        lax.fori_loop(0, count, step, 0)

    many, _ = halved(tiles[0], MANY)
    steps(0, MANY, many)
    few, _ = halved(tiles[0] - many * MANY + FEW - 1, FEW)
    steps(many * MANY, FEW, few)


def tile_scratch(heads, slots, tokens):
    query_side = pltpu.VMEM((heads * slots, tokens, BLOCK), jnp.bfloat16)
    key_side = pltpu.VMEM((heads * slots * (tokens // BLOCK), BLOCK, BLOCK), jnp.bfloat16)
    return [query_side] * 2 + [key_side] * 2 + [pltpu.VMEM((heads * slots, 8, tokens), jnp.float32)]


def stats_kernel(first, heads, slots, scaling, tiles, sink_ref, *refs):
    out_ref, q_all, g_all, k_all, v_all, rows = refs[-6:]
    query_side, key_side = (q_all, g_all), (k_all, v_all)
    spread([(0, 0, first, heads)], slots, refs, query_side, key_side)
    zero = jnp.zeros((1, out_ref.shape[2]), jnp.float32)
    for head in range(heads):
        for slot in range(slots):
            rows[head * slots + slot, 0:1, :] = zero + sink_ref[first + head]
            rows[head * slots + slot, 1:2, :] = zero
            rows[head * slots + slot, 2:3, :] = zero

    def work(query, one, two, scores, dprobs):
        old = rows[query, 0:1, :]
        top = jnp.maximum(old, jnp.max(scores, axis=0, keepdims=True) * scaling)
        parts = jnp.exp(scores * scaling - top)
        shrink = jnp.exp(old - top)
        rows[query, 0:1, :] = top
        rows[query, 1:2, :] = rows[query, 1:2, :] * shrink + jnp.sum(parts, axis=0, keepdims=True)
        rows[query, 2:3, :] = rows[query, 2:3, :] * shrink + jnp.sum(
            parts * dprobs, axis=0, keepdims=True
        )

    walk(tiles, query_side, key_side, work)
    for head in range(heads):
        for slot in range(slots):
            for kind in range(3):
                out_ref[head, pl.ds(kind * slots + slot, 1), :] = rows[
                    head * slots + slot, kind : kind + 1, :
                ]


def stats(tiles, sink, qd, kv, first, heads, scaling):
    slots, tokens = len(qd), qd[0].shape[2]
    rows = -(-3 * slots // 8) * 8
    return pl.pallas_call(
        lambda *refs: stats_kernel(first, heads, slots, scaling, *refs),
        in_specs=[pl.BlockSpec(memory_space=pltpu.SMEM)] * 2 + whole(2 * slots),
        out_specs=whole(1)[0],
        out_shape=jax.ShapeDtypeStruct((heads, rows, tokens), jnp.float32),
        scratch_shapes=tile_scratch(heads, slots, tokens),
        compiler_params=pltpu.CompilerParams(vmem_limit_bytes=VMEM_BYTES),
        cost_estimate=SMALL,
        name="row_stats",
    )(tiles, sink, *qd, *kv)


def settle(parts, sink):
    top = parts[0][0]
    for part in parts[1:]:
        top = jnp.maximum(top, part[0])
    total, mixed = jnp.exp(sink - top), jnp.zeros_like(top)
    for part in parts:
        grow = jnp.exp(part[0] - top)
        total = total + part[1] * grow
        mixed = mixed + part[2] * grow
    return top + jnp.log(total), mixed / total


def stat_place(slot, shift, side):
    return (slot // CORES - shift) % side * CORES + slot % CORES


def stat_rows(refs, head, slot, slots):
    side = len(refs)
    return [
        [ref[head, pl.ds(kind * slots + stat_place(slot, shift, side), 1), :] for kind in range(3)]
        for shift, ref in enumerate(refs)
    ]


def ordered(items, at, side):
    made = []
    for place in range(side):
        value = items[place]
        for own in range(1, side):
            value = jnp.where(at == own, items[(place - own) % side], value)
        made.append(value)
    return made


def coordinates(side):
    rest, core = halved(lax.axis_index("ctx"), CORES)
    row, col = halved(rest, side)
    return core, jnp.where(core == 0, col, row), jnp.where(core == 0, row, col)


def put_terms(ref, terms):
    high = terms.astype(jnp.bfloat16)
    rest = terms - high.astype(jnp.float32)
    middle = rest.astype(jnp.bfloat16)
    low = (rest - middle.astype(jnp.float32)).astype(jnp.bfloat16)
    row = lax.broadcasted_iota(jnp.int32, (EXTRA, BLOCK), 0)
    rows = [part.astype(jnp.float32) for part in (high, middle, low)]
    block = jnp.zeros((EXTRA, BLOCK), jnp.float32)
    for place, part in enumerate(rows):
        block = jnp.where(row == place, part, block)
    ref[...] = block.astype(jnp.bfloat16)


def get_terms(ref):
    block = ref[pl.ds(ref.shape[0] - EXTRA, EXTRA), :].astype(jnp.float32)
    return block[0:1] + block[1:2] + block[2:3]


def grads_kernel(spans, slots, side, scaling, joins, tiles, sink_ref, *refs):
    first, heads = spans[0][2], sum(span[-1] for span in spans)
    per_span = 2 * slots + side
    rest = refs[per_span * len(spans) :]
    remote = slots - CORES
    outs = rest[-11 - 2 * remote : -8]
    for before, place in zip(rest, joins):
        outs[place][: before.shape[0]] = before[...]
    dq_home, dkv_home, core_out = outs[:3]
    dq_out, dkv_out = outs[3 : 3 + remote], outs[3 + remote :]
    q_all, g_all, k_all, v_all, rows, dkeys, dvalues, dquery = rest[-8:]
    query_side, key_side = (q_all, g_all), (k_all, v_all)
    spread(spans, slots, refs, query_side, key_side)
    dkeys[...] = jnp.zeros_like(dkeys)
    dvalues[...] = jnp.zeros_like(dvalues)
    dquery[...] = jnp.zeros_like(dquery)
    place = 0
    for span, (_, offset, start, count) in enumerate(spans):
        stat_refs = refs[2 * slots * len(spans) + side * span :][:side]
        for head in range(count):
            for slot in range(slots):
                log_norm, row_delta = settle(
                    stat_rows(stat_refs, offset + head, slot, slots), sink_ref[start + head]
                )
                rows[place, 0:1, :] = log_norm
                rows[place, 1:2, :] = row_delta
                place += 1

    def work(query, one, two, scores, dprobs):
        weights = jnp.exp(scores * scaling - rows[query, 0:1, :])
        probs = weights.astype(jnp.bfloat16)
        dscores = (weights * (dprobs - rows[query, 1:2, :])).astype(jnp.bfloat16)
        dquery[query] += dot(paired(k_all, one, two), dscores, TN)
        dkey = dot(dscores, q_all[query], NN)
        dvalue = dot(probs, g_all[query], NN)
        dkeys[one] += dkey[:BLOCK]
        dkeys[two] += dkey[BLOCK:]
        dvalues[one] += dvalue[:BLOCK]
        dvalues[two] += dvalue[BLOCK:]

    walk(tiles, query_side, key_side, work)
    tokens = dq_home.shape[1]
    parts = tokens // BLOCK
    for head in range(heads):
        for slot in range(slots):
            place = head * slots + slot
            total = dquery[place].T * scaling
            if slot == 0:
                dq_home[head] = total
            elif slot < CORES:
                core_out[pl.ds((first + head) * 3 * tokens, tokens), :] = total.astype(jnp.bfloat16)
            else:
                dq_out[slot - CORES][pl.ds((first + head) * tokens, tokens), :] = total.astype(jnp.bfloat16)
            for part in range(parts):
                span = pl.ds(part * BLOCK, BLOCK)
                dkey = dkeys[place * parts + part] * scaling
                dvalue = dvalues[place * parts + part]
                if slot == 0:
                    dkv_home[head, 0, span, :] = dkey
                    dkv_home[head, 1, span, :] = dvalue
                    continue
                if slot < CORES:
                    ref, start = core_out, ((first + head) * 3 + 1) * tokens + part * BLOCK
                else:
                    ref, start = dkv_out[slot - CORES], head * 2 * tokens + part * BLOCK
                ref[pl.ds(start, BLOCK), :] = dkey.astype(jnp.bfloat16)
                ref[pl.ds(start + tokens, BLOCK), :] = dvalue.astype(jnp.bfloat16)


def grads(tiles, sink, qds, kvs, partials, before, after, spans, last, scaling):
    slots, tokens = len(qds[0]), qds[0][0].shape[2]
    first, heads = spans[0][2], sum(span[-1] for span in spans)
    side = len(partials[0])
    extra = EXTRA if last else 0
    remote = slots - CORES
    blocks = heads * slots * (tokens // BLOCK)
    low, high = jnp.bfloat16, jnp.float32
    joins = [] if before is None else list(range(2, 3 + remote))
    operands = [each for chunk, *_ in spans for each in qds[chunk] + kvs[chunk]]
    operands += [each for chunk, *_ in spans for each in partials[chunk]]
    operands += [before[place] for place in joins]
    shapes = [
        ((heads, tokens, BLOCK), high),
        ((heads, 2, tokens, BLOCK), high),
        (((first + heads) * 3 * tokens + extra, BLOCK), low),
    ]
    shapes += [(((first + heads) * tokens, BLOCK), low)] * remote
    shapes += [((heads * 2 * tokens + extra, BLOCK), low)] * remote
    return pl.pallas_call(
        lambda *refs: grads_kernel(spans, slots, side, scaling, joins, *refs),
        in_specs=[pl.BlockSpec(memory_space=pltpu.SMEM)] * 2
        + whole(len(operands))
        + [pl.BlockSpec(memory_space=pl.ANY)] * len(after),
        out_specs=whole(len(shapes)),
        out_shape=[jax.ShapeDtypeStruct(shape, kind) for shape, kind in shapes],
        scratch_shapes=tile_scratch(heads, slots, tokens)
        + [pltpu.VMEM((blocks, BLOCK, BLOCK), high)] * 2
        + [pltpu.VMEM((heads * slots, BLOCK, tokens), high)],
        compiler_params=pltpu.CompilerParams(vmem_limit_bytes=VMEM_BYTES),
        cost_estimate=pl.CostEstimate(
            flops=heads * 4 * 10**9, bytes_accessed=1, transcendentals=0
        ),
        name="gradients",
    )(tiles, sink, *operands, *after)


def gate(arrays, after):
    count = len(arrays)
    return pl.pallas_call(
        lambda *refs: None,
        in_specs=[pl.BlockSpec(memory_space=pl.ANY)] * (count + len(after)),
        out_specs=[pl.BlockSpec(memory_space=pl.ANY)] * count,
        out_shape=[jax.ShapeDtypeStruct(each.shape, each.dtype) for each in arrays],
        input_output_aliases={place: place for place in range(count)},
        compiler_params=pltpu.CompilerParams(vmem_limit_bytes=FEW_BYTES),
        cost_estimate=SMALL,
        name="gate",
    )(*arrays, *after)


def close_kernel(sizes, side, half, sums_ref, from_core, *refs):
    per = 2 + 2 * (side - 1)
    dq_far, refs = refs[: per - 2], refs[per - 2 :]
    *outs, sink_out = refs[per * len(sizes) :]
    core = lax.axis_index("ctx") % CORES
    first = 0
    for chunk, heads in enumerate(sizes):
        dq_home, dkv_home, *dkv_far = refs[per * chunk : per * (chunk + 1)]
        tokens = dq_home.shape[1]
        for head in range(heads):
            mine = pl.ds(pl.multiple_of(core * half + first, BLOCK), BLOCK)
            other = pl.ds(pl.multiple_of((1 - core) * half + first, BLOCK), BLOCK)
            for place, out in enumerate(outs):
                if place == 0:
                    parts = [dq_home[head]]
                    span = pl.ds(first // BLOCK * tokens, tokens)
                    parts += [ref[span, :] for ref in dq_far]
                else:
                    span = pl.ds((head * 2 + place - 1) * tokens, tokens)
                    parts = [dkv_home[head, place - 1]] + [ref[span, :] for ref in dkv_far]
                parts = [part.astype(jnp.float32) for part in parts]
                span = pl.ds((first // BLOCK * 3 + place) * tokens, tokens)
                start = from_core[span, :].astype(jnp.float32)
                out[0, :, mine] = sum(parts[1::2], parts[0]).astype(jnp.bfloat16)
                out[0, :, other] = sum(parts[2::2], start).astype(jnp.bfloat16)
            first += BLOCK
    half_heads = half // BLOCK
    _, at_query, at_key = coordinates(side)
    far = refs[per * len(sizes) - 2 * (side - 1) : per * len(sizes)]
    mine = [sums_ref[0:1, :]] + [get_terms(ref) for ref in far[0::2]]
    other = [get_terms(from_core)] + [get_terms(ref) for ref in far[1::2]]
    mine, other = sum(ordered(mine, at_key, side)), sum(ordered(other, at_query, side))
    low = jnp.where(core == 0, mine, other)
    high = pltpu.roll(jnp.where(core == 0, other, mine), half_heads, 1)
    lane = lax.broadcasted_iota(jnp.int32, (1, BLOCK), 1)
    sink_out[...] = jnp.where(lane < half_heads, low, high)[:, : 2 * half_heads]


def close(pieces, dq_far, from_core, sums, sizes, side, half, tokens):
    flat = [sums, from_core, *dq_far] + [piece for chunk in pieces for piece in chunk]
    return pl.pallas_call(
        lambda *refs: close_kernel(sizes, side, half, *refs),
        in_specs=whole(len(flat)),
        out_specs=whole(4),
        out_shape=[jax.ShapeDtypeStruct((1, tokens, 2 * half), jnp.bfloat16)] * 3
        + [jax.ShapeDtypeStruct((1, 2 * half // BLOCK), jnp.float32)],
        compiler_params=pltpu.CompilerParams(vmem_limit_bytes=VMEM_BYTES),
        cost_estimate=SMALL,
        name="closing_sums",
    )(*flat)


def halved(value, by):
    if by & (by - 1) == 0:
        return value >> (by.bit_length() - 1), value & (by - 1)
    return lax.div(value, jnp.int32(by)), lax.rem(value, jnp.int32(by))


def lists_kernel(spans, half_heads, side, per_group, listed, groups, *refs):
    slots = side * CORES
    asked, refs = refs[:slots], refs[slots:]
    own = (len(refs) - 2 - len(spans)) // 2
    outs, stages, spots, sems = refs[own : own + len(spans)], refs[own + len(spans) : -2], refs[-2], refs[-1]
    copies = [
        pltpu.make_async_copy(source, stage, sems.at[place])
        for place, (source, stage) in enumerate(zip(refs, stages))
    ]
    for copy in copies:
        copy.start()
    rest, core = halved(lax.axis_index("ctx"), CORES)
    row, col = halved(rest, side)

    def one_owner(owner, carry):
        rest, its_core = halved(owner, CORES)
        its_row, its_col = halved(rest, side)
        across = jnp.where(core == 0, its_col == col, its_row == row)
        along = jnp.where(core == 0, its_row - row, its_col - col)
        shift = jnp.where(along < 0, along + side, along)
        spot = (shift * CORES + jnp.where(its_core == core, 0, 1)) * per_group
        for part in range(per_group):
            spots[owner * per_group + part] = jnp.where(across, spot + part, -1)
        return carry

    lax.fori_loop(0, groups, one_owner, 0)
    for (first, heads), out in zip(spans, outs):

        def one_head(head, count, first=first, out=out):
            for slot in range(slots):
                query = head * slots + slot
                base = head * (slots * per_group)
                code = query
                for part in range(per_group // 2 if slot < CORES else 0):
                    left = base + slot * per_group + 2 * part
                    out[count] = query + (left << 8) + ((left + 2) << 16)
                    count = count + 1
                held = jnp.int32(0)
                blocks = asked[slot]
                for entry in range(listed):
                    spot = spots[blocks[core * half_heads + first + head, 0, entry]]
                    here = (spot >= 0).astype(jnp.int32)
                    place = base + spot
                    longer = jnp.where(held == 0, query + (place << 8), code + ((place + 1) << 16))
                    code = jnp.where(spot >= 0, longer, code)
                    out[count] = code
                    count = count + (here & held)
                    held = held ^ here
                count = count + held
            return count

        out[0] = lax.fori_loop(0, heads, one_head, jnp.int32(1)) - 1
    for copy in copies:
        copy.wait()


def tile_lists(asked, own, spans, half_heads, side, per_group, groups):
    slots, listed = len(asked), asked[0].shape[2]
    assert half_heads * slots * per_group < 255
    most = slots * ((listed + 1) // 2) + CORES * (per_group // 2)
    return pl.pallas_call(
        lambda *refs: lists_kernel(spans, half_heads, side, per_group, listed, groups, *refs),
        in_specs=[pl.BlockSpec(memory_space=pltpu.SMEM)] * slots
        + [pl.BlockSpec(memory_space=pl.ANY)] * len(own),
        out_specs=[pl.BlockSpec(memory_space=pltpu.SMEM)] * len(spans) + whole(len(own)),
        out_shape=[jax.ShapeDtypeStruct((heads * most + 8,), jnp.int32) for _, heads in spans]
        + [jax.ShapeDtypeStruct(each.shape, each.dtype) for each in own],
        scratch_shapes=[
            pltpu.SMEM((groups * per_group,), jnp.int32),
            pltpu.SemaphoreType.DMA((len(own),)),
        ],
        compiler_params=pltpu.CompilerParams(vmem_limit_bytes=VMEM_BYTES),
        cost_estimate=SMALL,
        name="tile_lists",
    )(*asked, *own)


def sink_kernel(sizes, slots, side, sink_ref, *refs):
    out = refs[-1]
    _, at_query, _ = coordinates(side)
    lane = lax.broadcasted_iota(jnp.int32, (1, BLOCK), 1)
    terms = jnp.zeros((1, BLOCK), jnp.float32)
    done = 0
    for chunk, heads in enumerate(sizes):
        stat_refs = refs[chunk * side : (chunk + 1) * side]
        for head in range(heads):
            sink = sink_ref[done]
            chips = []
            for shift in range(side):
                total = 0.0
                for cross in range(CORES):
                    rows = stat_rows(stat_refs, head, shift * CORES + cross, slots)
                    kinds = [ordered(kind, at_query, side) for kind in zip(*rows)]
                    log_norm, row_delta = settle(list(zip(*kinds)), sink)
                    total = total + jnp.exp(sink - log_norm) * row_delta
                chips.append(total)
            total = jnp.sum(sum(ordered(chips, at_query, side)))
            terms = terms - jnp.where(lane == done, total, 0.0)
            done += 1
    row = lax.broadcasted_iota(jnp.int32, out.shape, 0)
    out[...] = jnp.where(row == lax.axis_index("dp"), terms, 0.0)


def sink_terms(partials, sink, sizes, slots, side, after):
    operands = [part for parts in partials for part in parts]
    return pl.pallas_call(
        lambda *refs: sink_kernel(sizes, slots, side, *refs),
        in_specs=[pl.BlockSpec(memory_space=pltpu.SMEM)]
        + whole(len(operands))
        + [pl.BlockSpec(memory_space=pl.ANY)] * len(after),
        out_specs=whole(1)[0],
        out_shape=jax.ShapeDtypeStruct((lax.axis_size("dp"), BLOCK), jnp.float32),
        compiler_params=pltpu.CompilerParams(vmem_limit_bytes=FEW_BYTES),
        cost_estimate=SMALL,
        name="sink_terms",
    )(sink, *operands, *after)


def sink_mark(held, messages, arrays, after):
    count = len(messages)

    def kernel(held_ref, *refs):
        total = jnp.sum(held_ref[...], axis=0, keepdims=True)
        sum_ref, *outs = refs[count + len(arrays) + len(after) :]
        sum_ref[...] = jnp.broadcast_to(total, sum_ref.shape)
        for out in outs[:count]:
            put_terms(out, total)

    any_spec = pl.BlockSpec(memory_space=pl.ANY)
    ends = [
        pl.BlockSpec((EXTRA, BLOCK), lambda i, end=each.shape[0] // EXTRA - 1: (end, 0))
        for each in messages
    ]
    passed = [*messages, *arrays]
    return pl.pallas_call(
        kernel,
        grid=(1,),
        in_specs=[pl.BlockSpec(held.shape, lambda i: (0, 0))]
        + [any_spec] * (len(passed) + len(after)),
        out_specs=[pl.BlockSpec((8, BLOCK), lambda i: (0, 0))] + ends + [any_spec] * len(arrays),
        out_shape=[jax.ShapeDtypeStruct((8, BLOCK), jnp.float32)]
        + [jax.ShapeDtypeStruct(each.shape, each.dtype) for each in passed],
        input_output_aliases={place + 1: place + 1 for place in range(len(passed))},
        compiler_params=pltpu.CompilerParams(vmem_limit_bytes=FEW_BYTES),
        cost_estimate=SMALL,
        name="sink_mark",
    )(held, *passed, *after)


def sink_rounds():
    copies = lax.axis_size("dp")
    assert copies & (copies - 1) == 0
    rounds, step = [], 1
    while step < copies:
        radix = 4 if copies % (4 * step) == 0 else 2
        perms = [
            [(i, (i + part * step) % copies) for i in range(copies)] for part in range(1, radix)
        ]
        rounds.append(("dp", perms))
        step *= radix
    return rounds


def sink_round(held, axis, perms):
    return sum([lax.ppermute(held, axis, perm) for perm in perms], held)


def body(query_in, key_in, value_in, grad_out, key_blocks, sink_logits):
    groups = lax.axis_size("ctx")
    side = grid_side(groups)
    slots = side * CORES
    head_count = sink_logits.shape[0]
    tokens = query_in.shape[1]
    per_group = tokens // BLOCK
    assert key_blocks.shape[1] == 1 and query_in.shape[2] == head_count * BLOCK
    assert per_group % 2 == 0 and head_count % CORES == 0
    half_heads = head_count // 2
    half = half_heads * BLOCK
    scaling = 1.0 / math.sqrt(BLOCK)
    sizes = chunk_sizes(half_heads)
    starts = [sum(sizes[:i]) for i in range(len(sizes))]
    core = lax.axis_index("ctx") % CORES
    swap = gather_perm(groups, side, True, 0, 1)
    places = [(shift, cross) for shift in range(1, side) for cross in range(CORES)]
    remote = len(places)
    sink = jnp.where(core == 0, sink_logits[:half_heads], sink_logits[half_heads:])

    from_core = lax.ppermute(key_blocks, "ctx", swap)
    pair = jnp.concatenate([key_blocks, from_core], axis=1)
    asked = [key_blocks, from_core]
    for shift in range(1, side):
        came = lax.ppermute(pair, "ctx", gather_perm(groups, side, True, shift, 0))
        asked += [came[:, cross : cross + 1] for cross in range(CORES)]
    spans = list(zip(starts, sizes))
    parts = part_spans(sizes, part_sizes(half_heads))
    part_heads = [(part[0][2], sum(span[-1] for span in part)) for part in parts]
    fields = (query_in, grad_out, key_in, value_in)
    packed = pack(fields, sizes, half)
    own = [packed[4 * chunk + pair] for chunk in range(len(sizes)) for pair in range(2)]
    made = tile_lists(asked, own, spans + part_heads, half_heads, side, per_group, groups)
    tiles, own = made[: len(spans) + len(parts)], made[len(spans) + len(parts) :]
    from_core = lax.ppermute(packed[-1], "ctx", swap)
    qds, kvs = [], []
    for chunk in range(len(sizes)):
        here = packed[4 * chunk : 4 * chunk + 4]
        if chunk:
            here = gate(here[:3], [from_core]) + gate(here[3:], [from_core, *tiles])
        qd_own, kv_own, qd_oth, kv_oth = here
        qd, kv = [own[2 * chunk]], [own[2 * chunk + 1]]
        for shift, cross in places:
            perm = gather_perm(groups, side, True, shift, cross)
            qd.append(lax.ppermute(qd_oth if cross else qd_own, "ctx", perm))
            perm = gather_perm(groups, side, False, shift, cross)
            kv.append(lax.ppermute(kv_oth if cross else kv_own, "ctx", perm))
        qds.append(qd)
        kvs.append(kv)
    for qd, kv in zip(qds, kvs):
        qd.insert(1, from_core)
        kv.insert(1, from_core)

    partials = []
    for chunk, (first, heads) in enumerate(spans):
        partial = stats(tiles[chunk], sink, qds[chunk], kvs[chunk], first, heads, scaling)
        came = [
            lax.ppermute(partial, "ctx", gather_perm(groups, side, True, shift, 0))
            for shift in range(1, side)
        ]
        partials.append([partial] + came)
    rounds = sink_rounds()
    results, pieces, after = None, [], []
    for number, part in enumerate(parts):
        last = number == len(parts) - 1
        if number == 1 or last and not pieces:
            held = sink_terms(partials, sink, sizes, slots, side, [] if last else results[:1])
        if number >= 1 and rounds:
            after = [held]
            held = sink_round(held, *rounds.pop(0))
        results = grads(
            tiles[len(spans) + number],
            sink,
            qds,
            kvs,
            partials,
            results,
            after,
            part,
            last,
            scaling,
        )
        sent = results[3 + remote :]
        if last:
            for each in rounds:
                held = sink_round(held, *each)
            arriving = pieces[-1][2:] if pieces else []
            sums, core_out, *sent = sink_mark(held, [results[2], *sent], [], arriving)
        back = [
            lax.ppermute(value, "ctx", return_perm(groups, side, False, shift, cross))
            for value, (shift, cross) in zip(sent, places)
        ]
        pieces.append(list(results[:2]) + back)
    dq_far = [
        lax.ppermute(value, "ctx", return_perm(groups, side, True, shift, cross))
        for value, (shift, cross) in zip(results[3 : 3 + remote], places)
    ]
    from_core = lax.ppermute(core_out, "ctx", swap)
    grad_query, grad_key, grad_value, sinks = close(
        pieces, dq_far, from_core, sums, part_sizes(half_heads), side, half, tokens
    )
    grad_sink = sinks.reshape(head_count)
    return (grad_query, grad_key, grad_value, grad_sink)


def solution(mesh):
    tokens = P("dp", "ctx", None)
    return jax.shard_map(
        body,
        mesh=mesh,
        in_specs=(tokens, tokens, tokens, tokens, P(None, "ctx", None), P()),
        out_specs=(tokens, tokens, tokens, P()),
        check_vma=False,
    )
```

```python
import math

import jax
import jax.numpy as jnp
from jax import lax
from jax.experimental import pallas as pl
from jax.experimental.pallas import tpu as pltpu
from jax.sharding import PartitionSpec as P

BLOCK = 128
CORES = 2
FAR = -1e30
VMEM_BYTES = 24 * 1024 * 1024
FEW_BYTES = 2 * 1024 * 1024
MOST_BYTES = 62 * 1024 * 1024
MANY, FEW = 10, 5
EXTRA = 16
SMALL = pl.CostEstimate(flops=1, bytes_accessed=1, transcendentals=0)
NT = (((1,), (1,)), ((), ()))
NN = (((1,), (0,)), ((), ()))
TN = (((0,), (0,)), ((), ()))


def chunk_sizes(heads):
    return (heads - 1, 1) if heads > 1 else (1,)


def part_spans(sizes, part_sizes):
    where = [(chunk, offset) for chunk, size in enumerate(sizes) for offset in range(size)]
    parts, done = [], 0
    for count in part_sizes:
        spans = []
        for head in range(done, done + count):
            chunk, offset = where[head]
            if spans and spans[-1][0] == chunk:
                spans[-1] = spans[-1][:3] + (spans[-1][3] + 1,)
            else:
                spans.append((chunk, offset, head, 1))
        parts.append(spans)
        done += count
    return parts


def part_sizes(heads):
    return [heads - 1, 1] if heads > 1 else [1]


def grid_side(groups):
    side = math.isqrt(groups // CORES)
    assert CORES * side * side == groups
    return side


def moved(index, side, along_query, shift, cross):
    core, col, row = index % CORES, index // CORES % side, index // (CORES * side)
    along_col = (core == 0) == along_query
    if along_col:
        col = (col + shift) % side
    else:
        row = (row + shift) % side
    return (row * side + col) * CORES + (core ^ cross)


def gather_perm(groups, side, along_query, shift, cross):
    return [(moved(i, side, along_query, shift, cross), i) for i in range(groups)]


def return_perm(groups, side, along_query, shift, cross):
    return [(i, moved(i, side, along_query, shift, cross)) for i in range(groups)]


def dot(lhs, rhs, dims):
    return lax.dot_general(lhs, rhs, dims, preferred_element_type=jnp.float32)


def whole(count):
    return [pl.BlockSpec(memory_space=pltpu.VMEM)] * count


def pack_kernel(blocks, half, q_ref, g_ref, k_ref, v_ref, *rest):
    outs, (held, came, left) = rest[:-3], rest[-3:]
    core = lax.axis_index("ctx") % CORES
    arriving, leaving = [], []
    for count, (which, head, field, _) in enumerate(blocks):
        start = (core if which == 0 else 1 - core) * half + head * BLOCK
        columns = pl.ds(pl.multiple_of(start, BLOCK), BLOCK)
        copy = pltpu.make_async_copy(
            (q_ref, g_ref, k_ref, v_ref)[field].at[0, :, columns], held.at[count], came.at[count]
        )
        copy.start()
        arriving.append(copy)
    for count, (copy, (*_, targets)) in enumerate(zip(arriving, blocks)):
        copy.wait()
        for out, row, place in targets:
            leaving.append(
                pltpu.make_async_copy(
                    held.at[count], outs[out].at[row, place], left.at[len(leaving)]
                )
            )
            leaving[-1].start()
    for copy in leaving:
        copy.wait()


def pack(fields, sizes, half):
    tokens = fields[0].shape[1]
    blocks, first = [], 0
    for chunk, heads in enumerate(sizes):
        for row in range(heads):
            for which in range(2):
                for field in range(4):
                    targets = [(4 * chunk + 2 * which + field // 2, row, field % 2)]
                    targets += [(4 * len(sizes), first + row, field)] * which
                    blocks.append((which, first + row, field, targets))
        first += heads
    shapes = [(size, 2, tokens, BLOCK) for size in sizes for _ in range(4)]
    shapes.append((first, 4, tokens, BLOCK))
    return pl.pallas_call(
        lambda *refs: pack_kernel(blocks, half, *refs),
        in_specs=[pl.BlockSpec(memory_space=pl.ANY)] * 4,
        out_specs=[pl.BlockSpec(memory_space=pl.ANY)] * len(shapes),
        out_shape=[jax.ShapeDtypeStruct(shape, jnp.bfloat16) for shape in shapes],
        scratch_shapes=[
            pltpu.VMEM((len(blocks), tokens, BLOCK), jnp.bfloat16),
            pltpu.SemaphoreType.DMA((len(blocks),)),
            pltpu.SemaphoreType.DMA((sum(len(block[-1]) for block in blocks),)),
        ],
        compiler_params=pltpu.CompilerParams(vmem_limit_bytes=MOST_BYTES),
        cost_estimate=pl.CostEstimate(flops=4 * 10**9, bytes_accessed=1, transcendentals=0),
        name="pack",
    )(*fields)


def spread(spans, slots, refs, query_side, key_side):
    place = 0
    for span, (_, offset, first, heads) in enumerate(spans):
        here = refs[span * 2 * slots : (span + 1) * 2 * slots]
        qd_refs, kv_refs = here[:slots], here[slots:]
        parts = kv_refs[0].shape[2] // BLOCK
        for head in range(heads):
            for slot in range(slots):
                from_core = slot == 1
                row = head + (first if from_core else offset)
                for kind in range(2):
                    lead = kind + (2 if from_core else 0)
                    query_side[kind][place] = qd_refs[slot][row, kind]
                    for part in range(parts):
                        key_side[kind][place * parts + part] = kv_refs[slot][
                            row, lead, pl.ds(part * BLOCK, BLOCK), :
                        ]
                place += 1


def paired(ref, one, two):
    return jnp.concatenate([ref[one], ref[two]], axis=0)


def tile_products(tile, tiles, query_side, key_side):
    bound = tiles[0]
    real = tile < bound
    code = tiles[1 + jnp.minimum(tile, bound - 1)]
    query, one, two = code & 255, (code >> 8) & 255, (code >> 16) - 1
    both = real & (two >= 0)
    two = jnp.maximum(two, 0)
    raw = dot(paired(key_side[0], one, two), query_side[0][query], NT)
    scores = jnp.concatenate(
        [raw[:BLOCK] + jnp.where(real, 0.0, FAR), raw[BLOCK:] + jnp.where(both, 0.0, FAR)], axis=0
    )
    dprobs = dot(paired(key_side[1], one, two), query_side[1][query], NT)
    return query, one, two, scores, dprobs


def walk(tiles, query_side, key_side, work):
    def steps(start, size, count):
        def step(index, carry):
            made = [
                tile_products(start + size * index + i, tiles, query_side, key_side)
                for i in range(size)
            ]
            for one in made:
                work(*one)
            return carry

        lax.fori_loop(0, count, step, 0)

    many, _ = halved(tiles[0], MANY)
    steps(0, MANY, many)
    few, _ = halved(tiles[0] - many * MANY + FEW - 1, FEW)
    steps(many * MANY, FEW, few)


def tile_scratch(heads, slots, tokens):
    query_side = pltpu.VMEM((heads * slots, tokens, BLOCK), jnp.bfloat16)
    key_side = pltpu.VMEM((heads * slots * (tokens // BLOCK), BLOCK, BLOCK), jnp.bfloat16)
    return [query_side] * 2 + [key_side] * 2 + [pltpu.VMEM((heads * slots, 8, tokens), jnp.float32)]


def stats_kernel(first, heads, slots, scaling, tiles, sink_ref, *refs):
    out_ref, q_all, g_all, k_all, v_all, rows = refs[-6:]
    query_side, key_side = (q_all, g_all), (k_all, v_all)
    spread([(0, 0, first, heads)], slots, refs, query_side, key_side)
    zero = jnp.zeros((1, out_ref.shape[2]), jnp.float32)
    for head in range(heads):
        for slot in range(slots):
            rows[head * slots + slot, 0:1, :] = zero + sink_ref[first + head]
            rows[head * slots + slot, 1:2, :] = zero
            rows[head * slots + slot, 2:3, :] = zero

    def work(query, one, two, scores, dprobs):
        old = rows[query, 0:1, :]
        top = jnp.maximum(old, jnp.max(scores, axis=0, keepdims=True) * scaling)
        parts = jnp.exp(scores * scaling - top)
        shrink = jnp.exp(old - top)
        rows[query, 0:1, :] = top
        rows[query, 1:2, :] = rows[query, 1:2, :] * shrink + jnp.sum(parts, axis=0, keepdims=True)
        rows[query, 2:3, :] = rows[query, 2:3, :] * shrink + jnp.sum(
            parts * dprobs, axis=0, keepdims=True
        )

    walk(tiles, query_side, key_side, work)
    for head in range(heads):
        for slot in range(slots):
            for kind in range(3):
                out_ref[head, pl.ds(kind * slots + slot, 1), :] = rows[
                    head * slots + slot, kind : kind + 1, :
                ]


def stats(tiles, sink, qd, kv, first, heads, scaling):
    slots, tokens = len(qd), qd[0].shape[2]
    rows = -(-3 * slots // 8) * 8
    return pl.pallas_call(
        lambda *refs: stats_kernel(first, heads, slots, scaling, *refs),
        in_specs=[pl.BlockSpec(memory_space=pltpu.SMEM)] * 2 + whole(2 * slots),
        out_specs=whole(1)[0],
        out_shape=jax.ShapeDtypeStruct((heads, rows, tokens), jnp.float32),
        scratch_shapes=tile_scratch(heads, slots, tokens),
        compiler_params=pltpu.CompilerParams(vmem_limit_bytes=VMEM_BYTES),
        cost_estimate=SMALL,
        name="row_stats",
    )(tiles, sink, *qd, *kv)


def settle(parts, sink):
    top = parts[0][0]
    for part in parts[1:]:
        top = jnp.maximum(top, part[0])
    total, mixed = jnp.exp(sink - top), jnp.zeros_like(top)
    for part in parts:
        grow = jnp.exp(part[0] - top)
        total = total + part[1] * grow
        mixed = mixed + part[2] * grow
    return top + jnp.log(total), mixed / total


def stat_place(slot, shift, side):
    return (slot // CORES - shift) % side * CORES + slot % CORES


def stat_rows(refs, head, slot, slots):
    side = len(refs)
    return [
        [ref[head, pl.ds(kind * slots + stat_place(slot, shift, side), 1), :] for kind in range(3)]
        for shift, ref in enumerate(refs)
    ]


def ordered(items, at, side):
    made = []
    for place in range(side):
        value = items[place]
        for own in range(1, side):
            value = jnp.where(at == own, items[(place - own) % side], value)
        made.append(value)
    return made


def coordinates(side):
    rest, core = halved(lax.axis_index("ctx"), CORES)
    row, col = halved(rest, side)
    return core, jnp.where(core == 0, col, row), jnp.where(core == 0, row, col)


def put_terms(ref, terms):
    high = terms.astype(jnp.bfloat16)
    rest = terms - high.astype(jnp.float32)
    middle = rest.astype(jnp.bfloat16)
    low = (rest - middle.astype(jnp.float32)).astype(jnp.bfloat16)
    row = lax.broadcasted_iota(jnp.int32, (EXTRA, BLOCK), 0)
    rows = [part.astype(jnp.float32) for part in (high, middle, low)]
    block = jnp.zeros((EXTRA, BLOCK), jnp.float32)
    for place, part in enumerate(rows):
        block = jnp.where(row == place, part, block)
    ref[...] = block.astype(jnp.bfloat16)


def get_terms(ref):
    block = ref[pl.ds(ref.shape[0] - EXTRA, EXTRA), :].astype(jnp.float32)
    return block[0:1] + block[1:2] + block[2:3]


def grads_kernel(spans, slots, side, scaling, joins, tiles, sink_ref, *refs):
    first, heads = spans[0][2], sum(span[-1] for span in spans)
    per_span = 2 * slots + side
    rest = refs[per_span * len(spans) :]
    remote = slots - CORES
    outs = rest[-11 - 2 * remote : -8]
    for before, place in zip(rest, joins):
        outs[place][: before.shape[0]] = before[...]
    dq_home, dkv_home, core_out = outs[:3]
    dq_out, dkv_out = outs[3 : 3 + remote], outs[3 + remote :]
    q_all, g_all, k_all, v_all, rows, dkeys, dvalues, dquery = rest[-8:]
    query_side, key_side = (q_all, g_all), (k_all, v_all)
    spread(spans, slots, refs, query_side, key_side)
    dkeys[...] = jnp.zeros_like(dkeys)
    dvalues[...] = jnp.zeros_like(dvalues)
    dquery[...] = jnp.zeros_like(dquery)
    place = 0
    for span, (_, offset, start, count) in enumerate(spans):
        stat_refs = refs[2 * slots * len(spans) + side * span :][:side]
        for head in range(count):
            for slot in range(slots):
                log_norm, row_delta = settle(
                    stat_rows(stat_refs, offset + head, slot, slots), sink_ref[start + head]
                )
                rows[place, 0:1, :] = log_norm
                rows[place, 1:2, :] = row_delta
                place += 1

    def work(query, one, two, scores, dprobs):
        weights = jnp.exp(scores * scaling - rows[query, 0:1, :])
        probs = weights.astype(jnp.bfloat16)
        dscores = (weights * (dprobs - rows[query, 1:2, :])).astype(jnp.bfloat16)
        dquery[query] += dot(paired(k_all, one, two), dscores, TN)
        dkey = dot(dscores, q_all[query], NN)
        dvalue = dot(probs, g_all[query], NN)
        dkeys[one] += dkey[:BLOCK]
        dkeys[two] += dkey[BLOCK:]
        dvalues[one] += dvalue[:BLOCK]
        dvalues[two] += dvalue[BLOCK:]

    walk(tiles, query_side, key_side, work)
    tokens = dq_home.shape[1]
    parts = tokens // BLOCK
    for head in range(heads):
        for slot in range(slots):
            place = head * slots + slot
            total = dquery[place].T * scaling
            if slot == 0:
                dq_home[head] = total
            elif slot < CORES:
                core_out[pl.ds((first + head) * 3 * tokens, tokens), :] = total.astype(jnp.bfloat16)
            else:
                dq_out[slot - CORES][pl.ds((first + head) * tokens, tokens), :] = total.astype(jnp.bfloat16)
            for part in range(parts):
                span = pl.ds(part * BLOCK, BLOCK)
                dkey = dkeys[place * parts + part] * scaling
                dvalue = dvalues[place * parts + part]
                if slot == 0:
                    dkv_home[head, 0, span, :] = dkey
                    dkv_home[head, 1, span, :] = dvalue
                    continue
                if slot < CORES:
                    ref, start = core_out, ((first + head) * 3 + 1) * tokens + part * BLOCK
                else:
                    ref, start = dkv_out[slot - CORES], head * 2 * tokens + part * BLOCK
                ref[pl.ds(start, BLOCK), :] = dkey.astype(jnp.bfloat16)
                ref[pl.ds(start + tokens, BLOCK), :] = dvalue.astype(jnp.bfloat16)


def grads(tiles, sink, qds, kvs, partials, before, after, spans, last, scaling):
    slots, tokens = len(qds[0]), qds[0][0].shape[2]
    first, heads = spans[0][2], sum(span[-1] for span in spans)
    side = len(partials[0])
    extra = EXTRA if last else 0
    remote = slots - CORES
    blocks = heads * slots * (tokens // BLOCK)
    low, high = jnp.bfloat16, jnp.float32
    joins = [] if before is None else list(range(2, 3 + remote))
    operands = [each for chunk, *_ in spans for each in qds[chunk] + kvs[chunk]]
    operands += [each for chunk, *_ in spans for each in partials[chunk]]
    operands += [before[place] for place in joins]
    shapes = [
        ((heads, tokens, BLOCK), high),
        ((heads, 2, tokens, BLOCK), high),
        (((first + heads) * 3 * tokens + extra, BLOCK), low),
    ]
    shapes += [(((first + heads) * tokens, BLOCK), low)] * remote
    shapes += [((heads * 2 * tokens + extra, BLOCK), low)] * remote
    return pl.pallas_call(
        lambda *refs: grads_kernel(spans, slots, side, scaling, joins, *refs),
        in_specs=[pl.BlockSpec(memory_space=pltpu.SMEM)] * 2
        + whole(len(operands))
        + [pl.BlockSpec(memory_space=pl.ANY)] * len(after),
        out_specs=whole(len(shapes)),
        out_shape=[jax.ShapeDtypeStruct(shape, kind) for shape, kind in shapes],
        scratch_shapes=tile_scratch(heads, slots, tokens)
        + [pltpu.VMEM((blocks, BLOCK, BLOCK), high)] * 2
        + [pltpu.VMEM((heads * slots, BLOCK, tokens), high)],
        compiler_params=pltpu.CompilerParams(vmem_limit_bytes=VMEM_BYTES),
        cost_estimate=pl.CostEstimate(
            flops=heads * 4 * 10**9, bytes_accessed=1, transcendentals=0
        ),
        name="gradients",
    )(tiles, sink, *operands, *after)


def gate(arrays, after):
    count = len(arrays)
    return pl.pallas_call(
        lambda *refs: None,
        in_specs=[pl.BlockSpec(memory_space=pl.ANY)] * (count + len(after)),
        out_specs=[pl.BlockSpec(memory_space=pl.ANY)] * count,
        out_shape=[jax.ShapeDtypeStruct(each.shape, each.dtype) for each in arrays],
        input_output_aliases={place: place for place in range(count)},
        compiler_params=pltpu.CompilerParams(vmem_limit_bytes=FEW_BYTES),
        cost_estimate=SMALL,
        name="gate",
    )(*arrays, *after)


def close_kernel(sizes, side, half, sums_ref, from_core, *refs):
    per = 2 + 2 * (side - 1)
    dq_far, refs = refs[: per - 2], refs[per - 2 :]
    *outs, sink_out = refs[per * len(sizes) :]
    core = lax.axis_index("ctx") % CORES
    first = 0
    for chunk, heads in enumerate(sizes):
        dq_home, dkv_home, *dkv_far = refs[per * chunk : per * (chunk + 1)]
        tokens = dq_home.shape[1]
        for head in range(heads):
            mine = pl.ds(pl.multiple_of(core * half + first, BLOCK), BLOCK)
            other = pl.ds(pl.multiple_of((1 - core) * half + first, BLOCK), BLOCK)
            for place, out in enumerate(outs):
                if place == 0:
                    parts = [dq_home[head]]
                    span = pl.ds(first // BLOCK * tokens, tokens)
                    parts += [ref[span, :] for ref in dq_far]
                else:
                    span = pl.ds((head * 2 + place - 1) * tokens, tokens)
                    parts = [dkv_home[head, place - 1]] + [ref[span, :] for ref in dkv_far]
                parts = [part.astype(jnp.float32) for part in parts]
                span = pl.ds((first // BLOCK * 3 + place) * tokens, tokens)
                start = from_core[span, :].astype(jnp.float32)
                out[0, :, mine] = sum(parts[1::2], parts[0]).astype(jnp.bfloat16)
                out[0, :, other] = sum(parts[2::2], start).astype(jnp.bfloat16)
            first += BLOCK
    half_heads = half // BLOCK
    _, at_query, at_key = coordinates(side)
    far = refs[per * len(sizes) - 2 * (side - 1) : per * len(sizes)]
    mine = [sums_ref[0:1, :]] + [get_terms(ref) for ref in far[0::2]]
    other = [get_terms(from_core)] + [get_terms(ref) for ref in far[1::2]]
    mine, other = sum(ordered(mine, at_key, side)), sum(ordered(other, at_query, side))
    low = jnp.where(core == 0, mine, other)
    high = pltpu.roll(jnp.where(core == 0, other, mine), half_heads, 1)
    lane = lax.broadcasted_iota(jnp.int32, (1, BLOCK), 1)
    sink_out[...] = jnp.where(lane < half_heads, low, high)[:, : 2 * half_heads]


def close(pieces, dq_far, from_core, sums, sizes, side, half, tokens):
    flat = [sums, from_core, *dq_far] + [piece for chunk in pieces for piece in chunk]
    return pl.pallas_call(
        lambda *refs: close_kernel(sizes, side, half, *refs),
        in_specs=whole(len(flat)),
        out_specs=whole(4),
        out_shape=[jax.ShapeDtypeStruct((1, tokens, 2 * half), jnp.bfloat16)] * 3
        + [jax.ShapeDtypeStruct((1, 2 * half // BLOCK), jnp.float32)],
        compiler_params=pltpu.CompilerParams(vmem_limit_bytes=VMEM_BYTES),
        cost_estimate=SMALL,
        name="closing_sums",
    )(*flat)


def halved(value, by):
    if by & (by - 1) == 0:
        return value >> (by.bit_length() - 1), value & (by - 1)
    return lax.div(value, jnp.int32(by)), lax.rem(value, jnp.int32(by))


def lists_kernel(spans, half_heads, side, per_group, listed, groups, *refs):
    slots = side * CORES
    asked, refs = refs[:slots], refs[slots:]
    own = (len(refs) - 2 - len(spans)) // 2
    outs, stages, spots, sems = refs[own : own + len(spans)], refs[own + len(spans) : -2], refs[-2], refs[-1]
    copies = [
        pltpu.make_async_copy(source, stage, sems.at[place])
        for place, (source, stage) in enumerate(zip(refs, stages))
    ]
    for copy in copies:
        copy.start()
    rest, core = halved(lax.axis_index("ctx"), CORES)
    row, col = halved(rest, side)

    def one_owner(owner, carry):
        rest, its_core = halved(owner, CORES)
        its_row, its_col = halved(rest, side)
        across = jnp.where(core == 0, its_col == col, its_row == row)
        along = jnp.where(core == 0, its_row - row, its_col - col)
        shift = jnp.where(along < 0, along + side, along)
        spot = (shift * CORES + jnp.where(its_core == core, 0, 1)) * per_group
        for part in range(per_group):
            spots[owner * per_group + part] = jnp.where(across, spot + part, -1)
        return carry

    lax.fori_loop(0, groups, one_owner, 0)
    for (first, heads), out in zip(spans, outs):

        def one_head(head, count, first=first, out=out):
            for slot in range(slots):
                query = head * slots + slot
                base = head * (slots * per_group)
                code = query
                for part in range(per_group // 2 if slot < CORES else 0):
                    left = base + slot * per_group + 2 * part
                    out[count] = query + (left << 8) + ((left + 2) << 16)
                    count = count + 1
                held = jnp.int32(0)
                blocks = asked[slot]
                for entry in range(listed):
                    spot = spots[blocks[core * half_heads + first + head, 0, entry]]
                    here = (spot >= 0).astype(jnp.int32)
                    place = base + spot
                    longer = jnp.where(held == 0, query + (place << 8), code + ((place + 1) << 16))
                    code = jnp.where(spot >= 0, longer, code)
                    out[count] = code
                    count = count + (here & held)
                    held = held ^ here
                count = count + held
            return count

        out[0] = lax.fori_loop(0, heads, one_head, jnp.int32(1)) - 1
    for copy in copies:
        copy.wait()


def tile_lists(asked, own, spans, half_heads, side, per_group, groups):
    slots, listed = len(asked), asked[0].shape[2]
    assert half_heads * slots * per_group < 255
    most = slots * ((listed + 1) // 2) + CORES * (per_group // 2)
    return pl.pallas_call(
        lambda *refs: lists_kernel(spans, half_heads, side, per_group, listed, groups, *refs),
        in_specs=[pl.BlockSpec(memory_space=pltpu.SMEM)] * slots
        + [pl.BlockSpec(memory_space=pl.ANY)] * len(own),
        out_specs=[pl.BlockSpec(memory_space=pltpu.SMEM)] * len(spans) + whole(len(own)),
        out_shape=[jax.ShapeDtypeStruct((heads * most + 8,), jnp.int32) for _, heads in spans]
        + [jax.ShapeDtypeStruct(each.shape, each.dtype) for each in own],
        scratch_shapes=[
            pltpu.SMEM((groups * per_group,), jnp.int32),
            pltpu.SemaphoreType.DMA((len(own),)),
        ],
        compiler_params=pltpu.CompilerParams(vmem_limit_bytes=VMEM_BYTES),
        cost_estimate=SMALL,
        name="tile_lists",
    )(*asked, *own)


def sink_kernel(sizes, slots, side, sink_ref, *refs):
    out = refs[-1]
    _, at_query, _ = coordinates(side)
    lane = lax.broadcasted_iota(jnp.int32, (1, BLOCK), 1)
    terms = jnp.zeros((1, BLOCK), jnp.float32)
    done = 0
    for chunk, heads in enumerate(sizes):
        stat_refs = refs[chunk * side : (chunk + 1) * side]
        for head in range(heads):
            sink = sink_ref[done]
            chips = []
            for shift in range(side):
                total = 0.0
                for cross in range(CORES):
                    rows = stat_rows(stat_refs, head, shift * CORES + cross, slots)
                    kinds = [ordered(kind, at_query, side) for kind in zip(*rows)]
                    log_norm, row_delta = settle(list(zip(*kinds)), sink)
                    total = total + jnp.exp(sink - log_norm) * row_delta
                chips.append(total)
            total = jnp.sum(sum(ordered(chips, at_query, side)))
            terms = terms - jnp.where(lane == done, total, 0.0)
            done += 1
    row = lax.broadcasted_iota(jnp.int32, out.shape, 0)
    out[...] = jnp.where(row == lax.axis_index("dp"), terms, 0.0)


def sink_terms(partials, sink, sizes, slots, side, after):
    operands = [part for parts in partials for part in parts]
    return pl.pallas_call(
        lambda *refs: sink_kernel(sizes, slots, side, *refs),
        in_specs=[pl.BlockSpec(memory_space=pltpu.SMEM)]
        + whole(len(operands))
        + [pl.BlockSpec(memory_space=pl.ANY)] * len(after),
        out_specs=whole(1)[0],
        out_shape=jax.ShapeDtypeStruct((lax.axis_size("dp"), BLOCK), jnp.float32),
        compiler_params=pltpu.CompilerParams(vmem_limit_bytes=FEW_BYTES),
        cost_estimate=SMALL,
        name="sink_terms",
    )(sink, *operands, *after)


def sink_mark(held, messages, arrays, after):
    count = len(messages)

    def kernel(held_ref, *refs):
        total = jnp.sum(held_ref[...], axis=0, keepdims=True)
        sum_ref, *outs = refs[count + len(arrays) + len(after) :]
        sum_ref[...] = jnp.broadcast_to(total, sum_ref.shape)
        for out in outs[:count]:
            put_terms(out, total)

    any_spec = pl.BlockSpec(memory_space=pl.ANY)
    ends = [
        pl.BlockSpec((EXTRA, BLOCK), lambda i, end=each.shape[0] // EXTRA - 1: (end, 0))
        for each in messages
    ]
    passed = [*messages, *arrays]
    return pl.pallas_call(
        kernel,
        grid=(1,),
        in_specs=[pl.BlockSpec(held.shape, lambda i: (0, 0))]
        + [any_spec] * (len(passed) + len(after)),
        out_specs=[pl.BlockSpec((8, BLOCK), lambda i: (0, 0))] + ends + [any_spec] * len(arrays),
        out_shape=[jax.ShapeDtypeStruct((8, BLOCK), jnp.float32)]
        + [jax.ShapeDtypeStruct(each.shape, each.dtype) for each in passed],
        input_output_aliases={place + 1: place + 1 for place in range(len(passed))},
        compiler_params=pltpu.CompilerParams(vmem_limit_bytes=FEW_BYTES),
        cost_estimate=SMALL,
        name="sink_mark",
    )(held, *passed, *after)


def sink_rounds():
    copies = lax.axis_size("dp")
    assert copies & (copies - 1) == 0
    rounds, step = [], 1
    while step < copies:
        radix = 4 if copies % (4 * step) == 0 else 2
        perms = [
            [(i, (i + part * step) % copies) for i in range(copies)] for part in range(1, radix)
        ]
        rounds.append(("dp", perms))
        step *= radix
    return rounds


def sink_round(held, axis, perms):
    return sum([lax.ppermute(held, axis, perm) for perm in perms], held)


def body(query_in, key_in, value_in, grad_out, key_blocks, sink_logits):
    groups = lax.axis_size("ctx")
    side = grid_side(groups)
    slots = side * CORES
    head_count = sink_logits.shape[0]
    tokens = query_in.shape[1]
    per_group = tokens // BLOCK
    assert key_blocks.shape[1] == 1 and query_in.shape[2] == head_count * BLOCK
    assert per_group % 2 == 0 and head_count % CORES == 0
    half_heads = head_count // 2
    half = half_heads * BLOCK
    scaling = 1.0 / math.sqrt(BLOCK)
    sizes = chunk_sizes(half_heads)
    starts = [sum(sizes[:i]) for i in range(len(sizes))]
    core = lax.axis_index("ctx") % CORES
    swap = gather_perm(groups, side, True, 0, 1)
    places = [(shift, cross) for shift in range(1, side) for cross in range(CORES)]
    remote = len(places)
    sink = jnp.where(core == 0, sink_logits[:half_heads], sink_logits[half_heads:])

    from_core = lax.ppermute(key_blocks, "ctx", swap)
    pair = jnp.concatenate([key_blocks, from_core], axis=1)
    asked = [key_blocks, from_core]
    for shift in range(1, side):
        came = lax.ppermute(pair, "ctx", gather_perm(groups, side, True, shift, 0))
        asked += [came[:, cross : cross + 1] for cross in range(CORES)]
    spans = list(zip(starts, sizes))
    parts = part_spans(sizes, part_sizes(half_heads))
    part_heads = [(part[0][2], sum(span[-1] for span in part)) for part in parts]
    fields = (query_in, grad_out, key_in, value_in)
    packed = pack(fields, sizes, half)
    own = [packed[4 * chunk + pair] for chunk in range(len(sizes)) for pair in range(2)]
    made = tile_lists(asked, own, spans + part_heads, half_heads, side, per_group, groups)
    tiles, own = made[: len(spans) + len(parts)], made[len(spans) + len(parts) :]
    from_core = lax.ppermute(packed[-1], "ctx", swap)
    qds, kvs = [], []
    for chunk in range(len(sizes)):
        here = packed[4 * chunk : 4 * chunk + 4]
        if chunk:
            here = gate(here[:3], [from_core]) + gate(here[3:], [from_core, *tiles])
        qd_own, kv_own, qd_oth, kv_oth = here
        qd, kv = [own[2 * chunk]], [own[2 * chunk + 1]]
        for shift, cross in places:
            perm = gather_perm(groups, side, True, shift, cross)
            qd.append(lax.ppermute(qd_oth if cross else qd_own, "ctx", perm))
            perm = gather_perm(groups, side, False, shift, cross)
            kv.append(lax.ppermute(kv_oth if cross else kv_own, "ctx", perm))
        qds.append(qd)
        kvs.append(kv)
    for qd, kv in zip(qds, kvs):
        qd.insert(1, from_core)
        kv.insert(1, from_core)

    partials = []
    for chunk, (first, heads) in enumerate(spans):
        partial = stats(tiles[chunk], sink, qds[chunk], kvs[chunk], first, heads, scaling)
        came = [
            lax.ppermute(partial, "ctx", gather_perm(groups, side, True, shift, 0))
            for shift in range(1, side)
        ]
        partials.append([partial] + came)
    rounds = sink_rounds()
    results, pieces, after = None, [], []
    for number, part in enumerate(parts):
        last = number == len(parts) - 1
        if number == 1 or last and not pieces:
            held = sink_terms(partials, sink, sizes, slots, side, [] if last else results[:1])
        if number >= 1 and rounds:
            after = [held]
            held = sink_round(held, *rounds.pop(0))
        results = grads(
            tiles[len(spans) + number],
            sink,
            qds,
            kvs,
            partials,
            results,
            after,
            part,
            last,
            scaling,
        )
        sent = results[3 + remote :]
        if last:
            for each in rounds:
                held = sink_round(held, *each)
            arriving = pieces[-1][2:] if pieces else []
            sums, core_out, *sent = sink_mark(held, [results[2], *sent], [], arriving)
        back = [
            lax.ppermute(value, "ctx", return_perm(groups, side, False, shift, cross))
            for value, (shift, cross) in zip(sent, places)
        ]
        pieces.append(list(results[:2]) + back)
    dq_far = [
        lax.ppermute(value, "ctx", return_perm(groups, side, True, shift, cross))
        for value, (shift, cross) in zip(results[3 : 3 + remote], places)
    ]
    from_core = lax.ppermute(core_out, "ctx", swap)
    grad_query, grad_key, grad_value, sinks = close(
        pieces, dq_far, from_core, sums, part_sizes(half_heads), side, half, tokens
    )
    grad_sink = sinks.reshape(head_count)
    return (grad_query, grad_key, grad_value, grad_sink)


def solution(mesh):
    tokens = P("dp", "ctx", None)
    return jax.shard_map(
        body,
        mesh=mesh,
        in_specs=(tokens, tokens, tokens, tokens, P(None, "ctx", None), P()),
        out_specs=(tokens, tokens, tokens, P()),
        check_vma=False,
    )
```

```python
import math

import jax
import jax.numpy as jnp
from jax import lax
from jax.experimental import pallas as pl
from jax.experimental.pallas import tpu as pltpu
from jax.sharding import PartitionSpec as P

BLOCK = 128
CORES = 2
FAR = -1e30
VMEM_BYTES = 24 * 1024 * 1024
FEW_BYTES = 2 * 1024 * 1024
MOST_BYTES = 62 * 1024 * 1024
MANY, FEW = 10, 5
EXTRA = 16
SMALL = pl.CostEstimate(flops=1, bytes_accessed=1, transcendentals=0)
NT = (((1,), (1,)), ((), ()))
NN = (((1,), (0,)), ((), ()))
TN = (((0,), (0,)), ((), ()))


def chunk_sizes(heads):
    return (heads - 1, 1) if heads > 1 else (1,)


def part_spans(sizes, part_sizes):
    where = [(chunk, offset) for chunk, size in enumerate(sizes) for offset in range(size)]
    parts, done = [], 0
    for count in part_sizes:
        spans = []
        for head in range(done, done + count):
            chunk, offset = where[head]
            if spans and spans[-1][0] == chunk:
                spans[-1] = spans[-1][:3] + (spans[-1][3] + 1,)
            else:
                spans.append((chunk, offset, head, 1))
        parts.append(spans)
        done += count
    return parts


def part_sizes(heads):
    return [heads - 1, 1] if heads > 1 else [1]


def grid_side(groups):
    side = math.isqrt(groups // CORES)
    assert CORES * side * side == groups
    return side


def moved(index, side, along_query, shift, cross):
    core, col, row = index % CORES, index // CORES % side, index // (CORES * side)
    along_col = (core == 0) == along_query
    if along_col:
        col = (col + shift) % side
    else:
        row = (row + shift) % side
    return (row * side + col) * CORES + (core ^ cross)


def gather_perm(groups, side, along_query, shift, cross):
    return [(moved(i, side, along_query, shift, cross), i) for i in range(groups)]


def return_perm(groups, side, along_query, shift, cross):
    return [(i, moved(i, side, along_query, shift, cross)) for i in range(groups)]


def dot(lhs, rhs, dims):
    return lax.dot_general(lhs, rhs, dims, preferred_element_type=jnp.float32)


def whole(count):
    return [pl.BlockSpec(memory_space=pltpu.VMEM)] * count


def pack_kernel(blocks, half, q_ref, g_ref, k_ref, v_ref, *rest):
    outs, (held, came, left) = rest[:-3], rest[-3:]
    core = lax.axis_index("ctx") % CORES
    arriving, leaving = [], []
    for count, (which, head, field, _) in enumerate(blocks):
        start = (core if which == 0 else 1 - core) * half + head * BLOCK
        columns = pl.ds(pl.multiple_of(start, BLOCK), BLOCK)
        copy = pltpu.make_async_copy(
            (q_ref, g_ref, k_ref, v_ref)[field].at[0, :, columns], held.at[count], came.at[count]
        )
        copy.start()
        arriving.append(copy)
    for count, (copy, (*_, targets)) in enumerate(zip(arriving, blocks)):
        copy.wait()
        for out, row, place in targets:
            leaving.append(
                pltpu.make_async_copy(
                    held.at[count], outs[out].at[row, place], left.at[len(leaving)]
                )
            )
            leaving[-1].start()
    for copy in leaving:
        copy.wait()


def pack(fields, sizes, half):
    tokens = fields[0].shape[1]
    blocks, first = [], 0
    for chunk, heads in enumerate(sizes):
        for row in range(heads):
            for which in range(2):
                for field in range(4):
                    targets = [(4 * chunk + 2 * which + field // 2, row, field % 2)]
                    targets += [(4 * len(sizes), first + row, field)] * which
                    blocks.append((which, first + row, field, targets))
        first += heads
    shapes = [(size, 2, tokens, BLOCK) for size in sizes for _ in range(4)]
    shapes.append((first, 4, tokens, BLOCK))
    return pl.pallas_call(
        lambda *refs: pack_kernel(blocks, half, *refs),
        in_specs=[pl.BlockSpec(memory_space=pl.ANY)] * 4,
        out_specs=[pl.BlockSpec(memory_space=pl.ANY)] * len(shapes),
        out_shape=[jax.ShapeDtypeStruct(shape, jnp.bfloat16) for shape in shapes],
        scratch_shapes=[
            pltpu.VMEM((len(blocks), tokens, BLOCK), jnp.bfloat16),
            pltpu.SemaphoreType.DMA((len(blocks),)),
            pltpu.SemaphoreType.DMA((sum(len(block[-1]) for block in blocks),)),
        ],
        compiler_params=pltpu.CompilerParams(vmem_limit_bytes=MOST_BYTES),
        cost_estimate=pl.CostEstimate(flops=4 * 10**9, bytes_accessed=1, transcendentals=0),
        name="pack",
    )(*fields)


def spread(spans, slots, refs, query_side, key_side):
    place = 0
    for span, (_, offset, first, heads) in enumerate(spans):
        here = refs[span * 2 * slots : (span + 1) * 2 * slots]
        qd_refs, kv_refs = here[:slots], here[slots:]
        parts = kv_refs[0].shape[2] // BLOCK
        for head in range(heads):
            for slot in range(slots):
                from_core = slot == 1
                row = head + (first if from_core else offset)
                for kind in range(2):
                    lead = kind + (2 if from_core else 0)
                    query_side[kind][place] = qd_refs[slot][row, kind]
                    for part in range(parts):
                        key_side[kind][place * parts + part] = kv_refs[slot][
                            row, lead, pl.ds(part * BLOCK, BLOCK), :
                        ]
                place += 1


def paired(ref, one, two):
    return jnp.concatenate([ref[one], ref[two]], axis=0)


def tile_products(tile, tiles, query_side, key_side):
    bound = tiles[0]
    real = tile < bound
    code = tiles[1 + jnp.minimum(tile, bound - 1)]
    query, one, two = code & 255, (code >> 8) & 255, (code >> 16) - 1
    both = real & (two >= 0)
    two = jnp.maximum(two, 0)
    raw = dot(paired(key_side[0], one, two), query_side[0][query], NT)
    scores = jnp.concatenate(
        [raw[:BLOCK] + jnp.where(real, 0.0, FAR), raw[BLOCK:] + jnp.where(both, 0.0, FAR)], axis=0
    )
    dprobs = dot(paired(key_side[1], one, two), query_side[1][query], NT)
    return query, one, two, scores, dprobs


def walk(tiles, query_side, key_side, work):
    def steps(start, size, count):
        def step(index, carry):
            made = [
                tile_products(start + size * index + i, tiles, query_side, key_side)
                for i in range(size)
            ]
            for one in made:
                work(*one)
            return carry

        lax.fori_loop(0, count, step, 0)

    many, _ = halved(tiles[0], MANY)
    steps(0, MANY, many)
    few, _ = halved(tiles[0] - many * MANY + FEW - 1, FEW)
    steps(many * MANY, FEW, few)


def tile_scratch(heads, slots, tokens):
    query_side = pltpu.VMEM((heads * slots, tokens, BLOCK), jnp.bfloat16)
    key_side = pltpu.VMEM((heads * slots * (tokens // BLOCK), BLOCK, BLOCK), jnp.bfloat16)
    return [query_side] * 2 + [key_side] * 2 + [pltpu.VMEM((heads * slots, 8, tokens), jnp.float32)]


def stats_kernel(first, heads, slots, scaling, tiles, sink_ref, *refs):
    out_ref, q_all, g_all, k_all, v_all, rows = refs[-6:]
    query_side, key_side = (q_all, g_all), (k_all, v_all)
    spread([(0, 0, first, heads)], slots, refs, query_side, key_side)
    zero = jnp.zeros((1, out_ref.shape[2]), jnp.float32)
    for head in range(heads):
        for slot in range(slots):
            rows[head * slots + slot, 0:1, :] = zero + sink_ref[first + head]
            rows[head * slots + slot, 1:2, :] = zero
            rows[head * slots + slot, 2:3, :] = zero

    def work(query, one, two, scores, dprobs):
        old = rows[query, 0:1, :]
        top = jnp.maximum(old, jnp.max(scores, axis=0, keepdims=True) * scaling)
        parts = jnp.exp(scores * scaling - top)
        shrink = jnp.exp(old - top)
        rows[query, 0:1, :] = top
        rows[query, 1:2, :] = rows[query, 1:2, :] * shrink + jnp.sum(parts, axis=0, keepdims=True)
        rows[query, 2:3, :] = rows[query, 2:3, :] * shrink + jnp.sum(
            parts * dprobs, axis=0, keepdims=True
        )

    walk(tiles, query_side, key_side, work)
    for head in range(heads):
        for slot in range(slots):
            for kind in range(3):
                out_ref[head, pl.ds(kind * slots + slot, 1), :] = rows[
                    head * slots + slot, kind : kind + 1, :
                ]


def stats(tiles, sink, qd, kv, first, heads, scaling):
    slots, tokens = len(qd), qd[0].shape[2]
    rows = -(-3 * slots // 8) * 8
    return pl.pallas_call(
        lambda *refs: stats_kernel(first, heads, slots, scaling, *refs),
        in_specs=[pl.BlockSpec(memory_space=pltpu.SMEM)] * 2 + whole(2 * slots),
        out_specs=whole(1)[0],
        out_shape=jax.ShapeDtypeStruct((heads, rows, tokens), jnp.float32),
        scratch_shapes=tile_scratch(heads, slots, tokens),
        compiler_params=pltpu.CompilerParams(vmem_limit_bytes=VMEM_BYTES),
        cost_estimate=SMALL,
        name="row_stats",
    )(tiles, sink, *qd, *kv)


def settle(parts, sink):
    top = parts[0][0]
    for part in parts[1:]:
        top = jnp.maximum(top, part[0])
    total, mixed = jnp.exp(sink - top), jnp.zeros_like(top)
    for part in parts:
        grow = jnp.exp(part[0] - top)
        total = total + part[1] * grow
        mixed = mixed + part[2] * grow
    return top + jnp.log(total), mixed / total


def stat_place(slot, shift, side):
    return (slot // CORES - shift) % side * CORES + slot % CORES


def stat_rows(refs, head, slot, slots):
    side = len(refs)
    return [
        [ref[head, pl.ds(kind * slots + stat_place(slot, shift, side), 1), :] for kind in range(3)]
        for shift, ref in enumerate(refs)
    ]


def ordered(items, at, side):
    made = []
    for place in range(side):
        value = items[place]
        for own in range(1, side):
            value = jnp.where(at == own, items[(place - own) % side], value)
        made.append(value)
    return made


def coordinates(side):
    rest, core = halved(lax.axis_index("ctx"), CORES)
    row, col = halved(rest, side)
    return core, jnp.where(core == 0, col, row), jnp.where(core == 0, row, col)


def put_terms(ref, terms):
    high = terms.astype(jnp.bfloat16)
    rest = terms - high.astype(jnp.float32)
    middle = rest.astype(jnp.bfloat16)
    low = (rest - middle.astype(jnp.float32)).astype(jnp.bfloat16)
    row = lax.broadcasted_iota(jnp.int32, (EXTRA, BLOCK), 0)
    rows = [part.astype(jnp.float32) for part in (high, middle, low)]
    block = jnp.zeros((EXTRA, BLOCK), jnp.float32)
    for place, part in enumerate(rows):
        block = jnp.where(row == place, part, block)
    ref[...] = block.astype(jnp.bfloat16)


def get_terms(ref):
    block = ref[pl.ds(ref.shape[0] - EXTRA, EXTRA), :].astype(jnp.float32)
    return block[0:1] + block[1:2] + block[2:3]


def grads_kernel(spans, slots, side, scaling, joins, tiles, sink_ref, *refs):
    first, heads = spans[0][2], sum(span[-1] for span in spans)
    per_span = 2 * slots + side
    rest = refs[per_span * len(spans) :]
    remote = slots - CORES
    outs = rest[-11 - 2 * remote : -8]
    for before, place in zip(rest, joins):
        outs[place][: before.shape[0]] = before[...]
    dq_home, dkv_home, core_out = outs[:3]
    dq_out, dkv_out = outs[3 : 3 + remote], outs[3 + remote :]
    q_all, g_all, k_all, v_all, rows, dkeys, dvalues, dquery = rest[-8:]
    query_side, key_side = (q_all, g_all), (k_all, v_all)
    spread(spans, slots, refs, query_side, key_side)
    dkeys[...] = jnp.zeros_like(dkeys)
    dvalues[...] = jnp.zeros_like(dvalues)
    dquery[...] = jnp.zeros_like(dquery)
    place = 0
    for span, (_, offset, start, count) in enumerate(spans):
        stat_refs = refs[2 * slots * len(spans) + side * span :][:side]
        for head in range(count):
            for slot in range(slots):
                log_norm, row_delta = settle(
                    stat_rows(stat_refs, offset + head, slot, slots), sink_ref[start + head]
                )
                rows[place, 0:1, :] = log_norm
                rows[place, 1:2, :] = row_delta
                place += 1

    def work(query, one, two, scores, dprobs):
        weights = jnp.exp(scores * scaling - rows[query, 0:1, :])
        probs = weights.astype(jnp.bfloat16)
        dscores = (weights * (dprobs - rows[query, 1:2, :])).astype(jnp.bfloat16)
        dquery[query] += dot(paired(k_all, one, two), dscores, TN)
        dkey = dot(dscores, q_all[query], NN)
        dvalue = dot(probs, g_all[query], NN)
        dkeys[one] += dkey[:BLOCK]
        dkeys[two] += dkey[BLOCK:]
        dvalues[one] += dvalue[:BLOCK]
        dvalues[two] += dvalue[BLOCK:]

    walk(tiles, query_side, key_side, work)
    tokens = dq_home.shape[1]
    parts = tokens // BLOCK
    for head in range(heads):
        for slot in range(slots):
            place = head * slots + slot
            total = dquery[place].T * scaling
            if slot == 0:
                dq_home[head] = total
            elif slot < CORES:
                core_out[pl.ds((first + head) * 3 * tokens, tokens), :] = total.astype(jnp.bfloat16)
            else:
                dq_out[slot - CORES][pl.ds((first + head) * tokens, tokens), :] = total.astype(jnp.bfloat16)
            for part in range(parts):
                span = pl.ds(part * BLOCK, BLOCK)
                dkey = dkeys[place * parts + part] * scaling
                dvalue = dvalues[place * parts + part]
                if slot == 0:
                    dkv_home[head, 0, span, :] = dkey
                    dkv_home[head, 1, span, :] = dvalue
                    continue
                if slot < CORES:
                    ref, start = core_out, ((first + head) * 3 + 1) * tokens + part * BLOCK
                else:
                    ref, start = dkv_out[slot - CORES], head * 2 * tokens + part * BLOCK
                ref[pl.ds(start, BLOCK), :] = dkey.astype(jnp.bfloat16)
                ref[pl.ds(start + tokens, BLOCK), :] = dvalue.astype(jnp.bfloat16)


def grads(tiles, sink, qds, kvs, partials, before, after, spans, last, scaling):
    slots, tokens = len(qds[0]), qds[0][0].shape[2]
    first, heads = spans[0][2], sum(span[-1] for span in spans)
    side = len(partials[0])
    extra = EXTRA if last else 0
    remote = slots - CORES
    blocks = heads * slots * (tokens // BLOCK)
    low, high = jnp.bfloat16, jnp.float32
    joins = [] if before is None else list(range(2, 3 + remote))
    operands = [each for chunk, *_ in spans for each in qds[chunk] + kvs[chunk]]
    operands += [each for chunk, *_ in spans for each in partials[chunk]]
    operands += [before[place] for place in joins]
    shapes = [
        ((heads, tokens, BLOCK), high),
        ((heads, 2, tokens, BLOCK), high),
        (((first + heads) * 3 * tokens + extra, BLOCK), low),
    ]
    shapes += [(((first + heads) * tokens, BLOCK), low)] * remote
    shapes += [((heads * 2 * tokens + extra, BLOCK), low)] * remote
    return pl.pallas_call(
        lambda *refs: grads_kernel(spans, slots, side, scaling, joins, *refs),
        in_specs=[pl.BlockSpec(memory_space=pltpu.SMEM)] * 2
        + whole(len(operands))
        + [pl.BlockSpec(memory_space=pl.ANY)] * len(after),
        out_specs=whole(len(shapes)),
        out_shape=[jax.ShapeDtypeStruct(shape, kind) for shape, kind in shapes],
        scratch_shapes=tile_scratch(heads, slots, tokens)
        + [pltpu.VMEM((blocks, BLOCK, BLOCK), high)] * 2
        + [pltpu.VMEM((heads * slots, BLOCK, tokens), high)],
        compiler_params=pltpu.CompilerParams(vmem_limit_bytes=VMEM_BYTES),
        cost_estimate=pl.CostEstimate(
            flops=heads * 4 * 10**9, bytes_accessed=1, transcendentals=0
        ),
        name="gradients",
    )(tiles, sink, *operands, *after)


def gate(arrays, after):
    count = len(arrays)
    return pl.pallas_call(
        lambda *refs: None,
        in_specs=[pl.BlockSpec(memory_space=pl.ANY)] * (count + len(after)),
        out_specs=[pl.BlockSpec(memory_space=pl.ANY)] * count,
        out_shape=[jax.ShapeDtypeStruct(each.shape, each.dtype) for each in arrays],
        input_output_aliases={place: place for place in range(count)},
        compiler_params=pltpu.CompilerParams(vmem_limit_bytes=FEW_BYTES),
        cost_estimate=SMALL,
        name="gate",
    )(*arrays, *after)


def close_kernel(sizes, side, half, sums_ref, from_core, *refs):
    per = 2 + 2 * (side - 1)
    dq_far, refs = refs[: per - 2], refs[per - 2 :]
    *outs, sink_out = refs[per * len(sizes) :]
    core = lax.axis_index("ctx") % CORES
    first = 0
    for chunk, heads in enumerate(sizes):
        dq_home, dkv_home, *dkv_far = refs[per * chunk : per * (chunk + 1)]
        tokens = dq_home.shape[1]
        for head in range(heads):
            mine = pl.ds(pl.multiple_of(core * half + first, BLOCK), BLOCK)
            other = pl.ds(pl.multiple_of((1 - core) * half + first, BLOCK), BLOCK)
            for place, out in enumerate(outs):
                if place == 0:
                    parts = [dq_home[head]]
                    span = pl.ds(first // BLOCK * tokens, tokens)
                    parts += [ref[span, :] for ref in dq_far]
                else:
                    span = pl.ds((head * 2 + place - 1) * tokens, tokens)
                    parts = [dkv_home[head, place - 1]] + [ref[span, :] for ref in dkv_far]
                parts = [part.astype(jnp.float32) for part in parts]
                span = pl.ds((first // BLOCK * 3 + place) * tokens, tokens)
                start = from_core[span, :].astype(jnp.float32)
                out[0, :, mine] = sum(parts[1::2], parts[0]).astype(jnp.bfloat16)
                out[0, :, other] = sum(parts[2::2], start).astype(jnp.bfloat16)
            first += BLOCK
    half_heads = half // BLOCK
    _, at_query, at_key = coordinates(side)
    far = refs[per * len(sizes) - 2 * (side - 1) : per * len(sizes)]
    mine = [sums_ref[0:1, :]] + [get_terms(ref) for ref in reversed(far[0::2])]
    other = [get_terms(from_core)] + [get_terms(ref) for ref in reversed(far[1::2])]
    mine, other = sum(ordered(mine, at_key, side)), sum(ordered(other, at_query, side))
    low = jnp.where(core == 0, mine, other)
    high = pltpu.roll(jnp.where(core == 0, other, mine), half_heads, 1)
    lane = lax.broadcasted_iota(jnp.int32, (1, BLOCK), 1)
    sink_out[...] = jnp.where(lane < half_heads, low, high)[:, : 2 * half_heads]


def close(pieces, dq_far, from_core, sums, sizes, side, half, tokens):
    flat = [sums, from_core, *dq_far] + [piece for chunk in pieces for piece in chunk]
    return pl.pallas_call(
        lambda *refs: close_kernel(sizes, side, half, *refs),
        in_specs=whole(len(flat)),
        out_specs=whole(4),
        out_shape=[jax.ShapeDtypeStruct((1, tokens, 2 * half), jnp.bfloat16)] * 3
        + [jax.ShapeDtypeStruct((1, 2 * half // BLOCK), jnp.float32)],
        compiler_params=pltpu.CompilerParams(vmem_limit_bytes=VMEM_BYTES),
        cost_estimate=SMALL,
        name="closing_sums",
    )(*flat)


def halved(value, by):
    if by & (by - 1) == 0:
        return value >> (by.bit_length() - 1), value & (by - 1)
    return lax.div(value, jnp.int32(by)), lax.rem(value, jnp.int32(by))


def lists_kernel(spans, half_heads, side, per_group, listed, groups, *refs):
    slots = side * CORES
    asked, refs = refs[:slots], refs[slots:]
    own = (len(refs) - 2 - len(spans)) // 2
    outs, stages, spots, sems = refs[own : own + len(spans)], refs[own + len(spans) : -2], refs[-2], refs[-1]
    copies = [
        pltpu.make_async_copy(source, stage, sems.at[place])
        for place, (source, stage) in enumerate(zip(refs, stages))
    ]
    for copy in copies:
        copy.start()
    rest, core = halved(lax.axis_index("ctx"), CORES)
    row, col = halved(rest, side)

    def one_owner(owner, carry):
        rest, its_core = halved(owner, CORES)
        its_row, its_col = halved(rest, side)
        across = jnp.where(core == 0, its_col == col, its_row == row)
        along = jnp.where(core == 0, its_row - row, its_col - col)
        shift = jnp.where(along < 0, along + side, along)
        spot = (shift * CORES + jnp.where(its_core == core, 0, 1)) * per_group
        for part in range(per_group):
            spots[owner * per_group + part] = jnp.where(across, spot + part, -1)
        return carry

    lax.fori_loop(0, groups, one_owner, 0)
    for (first, heads), out in zip(spans, outs):

        def one_head(head, count, first=first, out=out):
            for slot in range(slots):
                query = head * slots + slot
                base = head * (slots * per_group)
                code = query
                for part in range(per_group // 2 if slot < CORES else 0):
                    left = base + slot * per_group + 2 * part
                    out[count] = query + (left << 8) + ((left + 2) << 16)
                    count = count + 1
                held = jnp.int32(0)
                blocks = asked[slot]
                for entry in range(listed):
                    spot = spots[blocks[core * half_heads + first + head, 0, entry]]
                    here = (spot >= 0).astype(jnp.int32)
                    place = base + spot
                    longer = jnp.where(held == 0, query + (place << 8), code + ((place + 1) << 16))
                    code = jnp.where(spot >= 0, longer, code)
                    out[count] = code
                    count = count + (here & held)
                    held = held ^ here
                count = count + held
            return count

        out[0] = lax.fori_loop(0, heads, one_head, jnp.int32(1)) - 1
    for copy in copies:
        copy.wait()


def tile_lists(asked, own, spans, half_heads, side, per_group, groups):
    slots, listed = len(asked), asked[0].shape[2]
    assert half_heads * slots * per_group < 255
    most = slots * ((listed + 1) // 2) + CORES * (per_group // 2)
    return pl.pallas_call(
        lambda *refs: lists_kernel(spans, half_heads, side, per_group, listed, groups, *refs),
        in_specs=[pl.BlockSpec(memory_space=pltpu.SMEM)] * slots
        + [pl.BlockSpec(memory_space=pl.ANY)] * len(own),
        out_specs=[pl.BlockSpec(memory_space=pltpu.SMEM)] * len(spans) + whole(len(own)),
        out_shape=[jax.ShapeDtypeStruct((heads * most + 8,), jnp.int32) for _, heads in spans]
        + [jax.ShapeDtypeStruct(each.shape, each.dtype) for each in own],
        scratch_shapes=[
            pltpu.SMEM((groups * per_group,), jnp.int32),
            pltpu.SemaphoreType.DMA((len(own),)),
        ],
        compiler_params=pltpu.CompilerParams(vmem_limit_bytes=VMEM_BYTES),
        cost_estimate=SMALL,
        name="tile_lists",
    )(*asked, *own)


def sink_kernel(sizes, slots, side, sink_ref, *refs):
    out = refs[-1]
    _, at_query, _ = coordinates(side)
    lane = lax.broadcasted_iota(jnp.int32, (1, BLOCK), 1)
    terms = jnp.zeros((1, BLOCK), jnp.float32)
    done = 0
    for chunk, heads in enumerate(sizes):
        stat_refs = refs[chunk * side : (chunk + 1) * side]
        for head in range(heads):
            sink = sink_ref[done]
            chips = []
            for shift in range(side):
                total = 0.0
                for cross in range(CORES):
                    rows = stat_rows(stat_refs, head, shift * CORES + cross, slots)
                    kinds = [ordered(kind, at_query, side) for kind in zip(*rows)]
                    log_norm, row_delta = settle(list(zip(*kinds)), sink)
                    total = total + jnp.exp(sink - log_norm) * row_delta
                chips.append(total)
            total = jnp.sum(sum(ordered(chips, at_query, side)))
            terms = terms - jnp.where(lane == done, total, 0.0)
            done += 1
    row = lax.broadcasted_iota(jnp.int32, out.shape, 0)
    out[...] = jnp.where(row == lax.axis_index("dp"), terms, 0.0)


def sink_terms(partials, sink, sizes, slots, side, after):
    operands = [part for parts in partials for part in parts]
    return pl.pallas_call(
        lambda *refs: sink_kernel(sizes, slots, side, *refs),
        in_specs=[pl.BlockSpec(memory_space=pltpu.SMEM)]
        + whole(len(operands))
        + [pl.BlockSpec(memory_space=pl.ANY)] * len(after),
        out_specs=whole(1)[0],
        out_shape=jax.ShapeDtypeStruct((lax.axis_size("dp"), BLOCK), jnp.float32),
        compiler_params=pltpu.CompilerParams(vmem_limit_bytes=FEW_BYTES),
        cost_estimate=SMALL,
        name="sink_terms",
    )(sink, *operands, *after)


def sink_mark(held, messages, arrays, after):
    count = len(messages)

    def kernel(held_ref, *refs):
        total = jnp.sum(held_ref[...], axis=0, keepdims=True)
        sum_ref, *outs = refs[count + len(arrays) + len(after) :]
        sum_ref[...] = jnp.broadcast_to(total, sum_ref.shape)
        for out in outs[:count]:
            put_terms(out, total)

    any_spec = pl.BlockSpec(memory_space=pl.ANY)
    ends = [
        pl.BlockSpec((EXTRA, BLOCK), lambda i, end=each.shape[0] // EXTRA - 1: (end, 0))
        for each in messages
    ]
    passed = [*messages, *arrays]
    return pl.pallas_call(
        kernel,
        grid=(1,),
        in_specs=[pl.BlockSpec(held.shape, lambda i: (0, 0))]
        + [any_spec] * (len(passed) + len(after)),
        out_specs=[pl.BlockSpec((8, BLOCK), lambda i: (0, 0))] + ends + [any_spec] * len(arrays),
        out_shape=[jax.ShapeDtypeStruct((8, BLOCK), jnp.float32)]
        + [jax.ShapeDtypeStruct(each.shape, each.dtype) for each in passed],
        input_output_aliases={place + 1: place + 1 for place in range(len(passed))},
        compiler_params=pltpu.CompilerParams(vmem_limit_bytes=FEW_BYTES),
        cost_estimate=SMALL,
        name="sink_mark",
    )(held, *passed, *after)


def sink_rounds():
    copies = lax.axis_size("dp")
    assert copies & (copies - 1) == 0
    rounds, step = [], 1
    while step < copies:
        radix = 4 if copies % (4 * step) == 0 else 2
        perms = [
            [(i, (i + part * step) % copies) for i in range(copies)] for part in range(1, radix)
        ]
        rounds.append(("dp", perms))
        step *= radix
    return rounds


def sink_round(held, axis, perms):
    return sum([lax.ppermute(held, axis, perm) for perm in perms], held)


def body(query_in, key_in, value_in, grad_out, key_blocks, sink_logits):
    groups = lax.axis_size("ctx")
    side = grid_side(groups)
    slots = side * CORES
    head_count = sink_logits.shape[0]
    tokens = query_in.shape[1]
    per_group = tokens // BLOCK
    assert key_blocks.shape[1] == 1 and query_in.shape[2] == head_count * BLOCK
    assert per_group % 2 == 0 and head_count % CORES == 0
    half_heads = head_count // 2
    half = half_heads * BLOCK
    scaling = 1.0 / math.sqrt(BLOCK)
    sizes = chunk_sizes(half_heads)
    starts = [sum(sizes[:i]) for i in range(len(sizes))]
    core = lax.axis_index("ctx") % CORES
    swap = gather_perm(groups, side, True, 0, 1)
    places = [(shift, cross) for shift in range(1, side) for cross in range(CORES)]
    remote = len(places)
    sink = jnp.where(core == 0, sink_logits[:half_heads], sink_logits[half_heads:])

    from_core = lax.ppermute(key_blocks, "ctx", swap)
    pair = jnp.concatenate([key_blocks, from_core], axis=1)
    asked = [key_blocks, from_core]
    for shift in range(1, side):
        came = lax.ppermute(pair, "ctx", gather_perm(groups, side, True, shift, 0))
        asked += [came[:, cross : cross + 1] for cross in range(CORES)]
    spans = list(zip(starts, sizes))
    parts = part_spans(sizes, part_sizes(half_heads))
    part_heads = [(part[0][2], sum(span[-1] for span in part)) for part in parts]
    fields = (query_in, grad_out, key_in, value_in)
    packed = pack(fields, sizes, half)
    own = [packed[4 * chunk + pair] for chunk in range(len(sizes)) for pair in range(2)]
    made = tile_lists(asked, own, spans + part_heads, half_heads, side, per_group, groups)
    tiles, own = made[: len(spans) + len(parts)], made[len(spans) + len(parts) :]
    from_core = lax.ppermute(packed[-1], "ctx", swap)
    qds, kvs = [], []
    for chunk in range(len(sizes)):
        here = packed[4 * chunk : 4 * chunk + 4]
        if chunk:
            here = gate(here[:3], [from_core]) + gate(here[3:], [from_core, *tiles])
        qd_own, kv_own, qd_oth, kv_oth = here
        qd, kv = [own[2 * chunk]], [own[2 * chunk + 1]]
        for shift, cross in places:
            perm = gather_perm(groups, side, True, shift, cross)
            qd.append(lax.ppermute(qd_oth if cross else qd_own, "ctx", perm))
            perm = gather_perm(groups, side, False, shift, cross)
            kv.append(lax.ppermute(kv_oth if cross else kv_own, "ctx", perm))
        qds.append(qd)
        kvs.append(kv)
    for qd, kv in zip(qds, kvs):
        qd.insert(1, from_core)
        kv.insert(1, from_core)

    partials = []
    for chunk, (first, heads) in enumerate(spans):
        partial = stats(tiles[chunk], sink, qds[chunk], kvs[chunk], first, heads, scaling)
        came = [
            lax.ppermute(partial, "ctx", gather_perm(groups, side, True, shift, 0))
            for shift in range(1, side)
        ]
        partials.append([partial] + came)
    rounds = sink_rounds()
    results, pieces, after = None, [], []
    for number, part in enumerate(parts):
        last = number == len(parts) - 1
        if number == 1 or last and not pieces:
            held = sink_terms(partials, sink, sizes, slots, side, [] if last else results[:1])
        if number >= 1 and rounds:
            after = [held]
            held = sink_round(held, *rounds.pop(0))
        results = grads(
            tiles[len(spans) + number],
            sink,
            qds,
            kvs,
            partials,
            results,
            after,
            part,
            last,
            scaling,
        )
        sent = results[3 + remote :]
        if last:
            for each in rounds:
                held = sink_round(held, *each)
            arriving = pieces[-1][2:] if pieces else []
            sums, core_out, *sent = sink_mark(held, [results[2], *sent], [], arriving)
        back = [
            lax.ppermute(value, "ctx", return_perm(groups, side, False, shift, cross))
            for value, (shift, cross) in zip(sent, places)
        ]
        pieces.append(list(results[:2]) + back)
    dq_far = [
        lax.ppermute(value, "ctx", return_perm(groups, side, True, shift, cross))
        for value, (shift, cross) in zip(results[3 : 3 + remote], places)
    ]
    from_core = lax.ppermute(core_out, "ctx", swap)
    grad_query, grad_key, grad_value, sinks = close(
        pieces, dq_far, from_core, sums, part_sizes(half_heads), side, half, tokens
    )
    grad_sink = sinks.reshape(head_count)
    return (grad_query, grad_key, grad_value, grad_sink)


def solution(mesh):
    tokens = P("dp", "ctx", None)
    return jax.shard_map(
        body,
        mesh=mesh,
        in_specs=(tokens, tokens, tokens, tokens, P(None, "ctx", None), P()),
        out_specs=(tokens, tokens, tokens, P()),
        check_vma=False,
    )
```
